256 devices in a mesh: var: 8 (over x, z_hi), band: 32 (over z_lo, y, core).
Axes of the slice: x: 4, y: 4, z: 8 (z_hi: 2, z_lo: 4; z = z_hi * 4 + z_lo), core: 2. Of those that a mesh axis runs over, the one named last changes fastest.
Arguments:
- fields: bfloat16 [4, 80, 512, 1440], P(None, 'var', 'band'), may hold values from -6 to 6
- var_ids: int32 [80], P('var'), may hold values from 0 to 79, each once
- var_shift: float32 [80], replicated, may hold values from -4 to 4
- var_scale: float32 [80], replicated, may hold values from 0.3 to 3
- patch_weight: bfloat16 [80, 64, 1024], P('var'), may hold values from -1.25 to 1.25
- pos_table: float32 [16, 45, 1024], P(None, None, 'var'), may hold values from -5 to 5
- layer_norm_gain: float32 [1024], P('var'), may hold values from 0.5 to 1.5
- layer_norm_bias: float32 [1024], P('var'), may hold values from -2 to 2
- order: int32 [46080], P('band'), may hold values from 0 to 46079, as said below
- grad_out: bfloat16 [46080, 1024], P('band', 'var'), may hold values from -0.059814453 to 0.059814453
Outputs:
- embed: bfloat16 [46080, 1024], P('band', 'var')
- grad_weight: float32 [5120, 1024], P(('var', 'band'))
- grad_table: float32 [16, 45, 1024], P(None, None, 'var')
- grad_gain: float32 [1024], P('var')
- grad_bias: float32 [1024], P('var')
The draws below stay inside these ranges and needn't reach their ends.
Inputs may be any that keep to these rules, and one draw needn't show every extreme that they name: `var_ids`: A permutation of the 80 variables. `order`: A permutation of the 46080 positions; each block of 1440 positions receives exactly 45 tokens from the 1440 tokens of every band.
All inputs are finite; a program needn't handle non-finite values.
Results may differ from the reference program's by a relative error of at most 0.011.
Values may be sent and summed in bfloat16 or wider, within the bound.
A program may use at most 128 MiB of HBM per device.

```python
import math
import jax
import jax.numpy as jnp
from jax import lax

E = 1024
VAR_DEV = 10
PATCH = 64
PC = 180
PR_DEV = 2
SAMPLES = 4
VARS = 80
LAT = 512
LON = 1440
TB = 1440
SEQ = 46080
TLAT = 16
TLON = 45
N_VAR = 8
N_BAND = 32


def draw_patch_weight(key, part):
    key = jax.random.fold_in(key, 5)
    first, second = jax.random.split(key)
    column = jnp.exp(jax.random.uniform(second, (1, 1, E), jnp.float32, 0.0, math.log(10.0))) / math.sqrt(10.0)
    base = jnp.clip(jax.random.normal(first, (VARS, PATCH, E), jnp.float32), -6.0, 6.0)
    return (base * column * (VARS * PATCH) ** (-0.5)).astype(jnp.bfloat16)


def draw_order(key, part):
    key = jax.random.fold_in(key, 11)
    shards = SEQ // TB
    per = TB // shards
    first, second = jax.random.split(key)
    from_perm = jax.vmap(lambda k: jax.random.permutation(k, TB))(jax.random.split(first, shards))
    into_perm = jax.vmap(lambda k: jax.random.permutation(k, TB))(jax.random.split(second, shards))
    values = jnp.arange(shards)[:, None, None] * TB + into_perm.reshape(shards, shards, per)
    values = values.transpose(1, 0, 2).reshape(shards, TB).astype(jnp.int32)
    rows_idx = jnp.arange(shards)[:, None]
    placed = jnp.zeros((shards, TB), jnp.int32).at[rows_idx, from_perm].set(values)
    return placed.reshape(SEQ)


def levels(key, extent, cuts, low, largest):
    gain = 1.0
    for axis_at, parts in cuts:
        draws = jax.random.uniform(jax.random.fold_in(jax.random.fold_in(key, 6), axis_at), (parts,), jnp.float32, low / len(cuts), largest / len(cuts))
        gain = gain * jnp.repeat(jnp.exp(draws), extent[axis_at] // parts).reshape((-1,) + (1,) * (len(extent) - 1 - axis_at))
    return gain


def scatter_about(key, dims, scale, limit, cuts=(), dtype=jnp.bfloat16):
    result = jax.random.normal(key, dims, jnp.float32) * scale
    if len(cuts) > 0:
        result = levels(key, dims, cuts, -0.22, 0.18) * result
    return jnp.clip(result, min=-limit, max=limit).astype(dtype)


def setup_inputs(seed: int = 0) -> dict:
    key_of = jax.random.split(jax.random.key(seed), 11)
    fields = scatter_about(key_of[0], (SAMPLES, VARS, LAT, LON), 1.0, 6.0, ((1, 8), (2, 32)))
    var_ids = jax.random.permutation(key_of[1], VARS).astype(jnp.int32)
    var_shift = scatter_about(key_of[2], (VARS,), 1.0, 4.0, (), jnp.float32)
    var_scale = jnp.clip(jnp.exp(jax.random.uniform(key_of[3], (VARS,), jnp.float32, math.log(0.3), math.log(3.0))), 0.3, 3.0)
    patch_weight = draw_patch_weight(jax.random.fold_in(key_of[10], 71), 0)
    pos_table = scatter_about(key_of[5], (TLAT, TLON, E), 1.0, 5.0, ((2, 8),), jnp.float32)
    layer_norm_gain = jnp.clip(1.0 + 0.1 * jax.random.normal(key_of[6], (E,), jnp.float32), 0.5, 1.5)
    layer_norm_bias = scatter_about(key_of[7], (E,), 0.3, 2.0, ((0, 8),), jnp.float32)
    order = draw_order(jax.random.fold_in(key_of[10], 71), 0)
    grad_out = scatter_about(key_of[9], (SEQ, E), 0.01, 0.059814453, ((0, 32), (1, 8)))
    return dict(fields=fields, var_ids=var_ids, var_shift=var_shift, var_scale=var_scale, patch_weight=patch_weight, pos_table=pos_table, layer_norm_gain=layer_norm_gain, layer_norm_bias=layer_norm_bias, order=order, grad_out=grad_out)


eps = 1e-05
stride_ratio = 4.0

def blend(lat_row, lon_col, tlat, tlon):
    u = jnp.clip((lat_row.astype(jnp.float32) + 0.5) / stride_ratio - 0.5, 0.0, tlat - 1.0)
    w = (lon_col.astype(jnp.float32) + 0.5) / stride_ratio - 0.5
    lat_w = jnp.maximum(1.0 - jnp.abs(u[:, None] - jnp.arange(tlat).astype(jnp.float32)[None, :]), 0.0)
    dist = jnp.abs(w[:, None] - jnp.arange(tlon).astype(jnp.float32)[None, :])
    dist = jnp.minimum(dist, tlon - dist)
    lon_w = jnp.maximum(1.0 - dist, 0.0)
    return (lat_w[:, :, None] * lon_w[:, None, :]).reshape(lat_row.shape[0], tlat * tlon)

def locate(source, tokens_band, rows_band, columns):
    inner = source % tokens_band
    band_of = source // tokens_band
    return (band_of * rows_band + inner // columns % rows_band, inner % columns)

def reference(fields, var_ids, var_shift, var_scale, patch_weight, pos_table, layer_norm_gain, layer_norm_bias, order, grad_out):
    tb = SAMPLES * PR_DEV * PC
    shift = var_shift[var_ids]
    scale = var_scale[var_ids]
    weights = patch_weight.reshape(N_VAR, VAR_DEV * PATCH, E).astype(jnp.float32)
    table_flat = pos_table.reshape(TLAT * TLON, E)
    grad_tiles = grad_out[order]

    def tile_step(carry, band):
        grad_w, grad_t, gain_gradient, grad_b = carry
        block = lax.dynamic_slice_in_dim(fields, band * PR_DEV * 8, PR_DEV * 8, 2)
        normed = ((block.astype(jnp.float32) - shift[None, :, None, None]) * scale[None, :, None, None]).astype(jnp.bfloat16)
        patches = normed.reshape(SAMPLES, VARS, PR_DEV, 8, PC, 8).transpose(0, 2, 4, 1, 3, 5).reshape(tb, VARS * PATCH)
        grouped = patches.reshape(tb, N_VAR, VAR_DEV * PATCH).astype(jnp.float32)
        partial_value = jnp.einsum('tgk,gke->gte', grouped, weights).astype(jnp.bfloat16)
        summed = lax.optimization_barrier(jnp.sum(partial_value.astype(jnp.float32), 0))
        source = band * tb + jnp.arange(tb)
        lat_row, lon_col = locate(source, tb, PR_DEV, PC)
        mix = blend(lat_row, lon_col, TLAT, TLON)
        prenorm_input = summed + jnp.dot(mix, table_flat, precision=lax.Precision.HIGHEST)
        feature_mean = lax.optimization_barrier(jnp.mean(prenorm_input, 1))
        spread = lax.optimization_barrier(jnp.mean(prenorm_input * prenorm_input, 1)) - feature_mean * feature_mean
        inverse_deviation = lax.rsqrt(spread + eps)
        normalized_input = (prenorm_input - feature_mean[:, None]) * inverse_deviation[:, None]
        output_tile_block = (normalized_input * layer_norm_gain + layer_norm_bias).astype(jnp.bfloat16)
        upstream_gradient = lax.dynamic_slice_in_dim(grad_tiles, band * tb, tb, 0).astype(jnp.float32)
        scaled_values = upstream_gradient * layer_norm_gain
        preceding_gradient = inverse_deviation[:, None] * (scaled_values - lax.optimization_barrier(jnp.mean(scaled_values, 1, keepdims=True)) - normalized_input * lax.optimization_barrier(jnp.mean(scaled_values * normalized_input, 1, keepdims=True)))
        preceding_gradient = preceding_gradient.astype(jnp.bfloat16)
        grad_w = grad_w + jnp.dot(patches.T, preceding_gradient, preferred_element_type=jnp.float32)
        grad_t = grad_t + jnp.dot(mix.T, preceding_gradient.astype(jnp.float32), precision=lax.Precision.HIGHEST)
        gain_gradient = gain_gradient + lax.optimization_barrier(jnp.sum(upstream_gradient * normalized_input, 0))
        grad_b = grad_b + lax.optimization_barrier(jnp.sum(upstream_gradient, 0))
        return ((grad_w, grad_t, gain_gradient, grad_b), output_tile_block)
    start = (jnp.zeros((VARS * PATCH, E), jnp.float32), jnp.zeros((TLAT * TLON, E), jnp.float32), jnp.zeros((E,), jnp.float32), jnp.zeros((E,), jnp.float32))
    totals, tiles = lax.scan(tile_step, start, jnp.arange(N_BAND))
    embed = jnp.zeros((SEQ, E), jnp.bfloat16).at[order].set(tiles.reshape(SEQ, E))
    return (embed, totals[0], totals[1].reshape(TLAT, TLON, E), totals[2], totals[3])
```

```python
import functools

import jax
import jax.numpy as jnp
from jax import lax
from jax.experimental import pallas as pl
from jax.experimental.pallas import tpu as pltpu
from jax.sharding import PartitionSpec as P

EPS = 1e-05
T = 1536
LANES = 128
NB = 32
NV = 8
PER = 48
USED = 45
E = 1024
HALF = T // 2
PIECE = 256
PIECES = (0, 3, 1, 4, 2, 5)
F32 = jnp.float32
BF16 = jnp.bfloat16
HI = lax.Precision.HIGHEST


def iota(shape, dim):
    return lax.broadcasted_iota(jnp.int32, shape, dim)


def onehot(cond):
    return jnp.where(cond, 1.0, 0.0).astype(BF16)


def dot(a, b):
    return jnp.dot(a, b, preferred_element_type=F32)


def remote(src, dst, send, recv, v, b):
    return pltpu.make_async_remote_copy(
        src_ref=src,
        dst_ref=dst,
        send_sem=send,
        recv_sem=recv,
        device_id=(v, b),
        device_id_type=pl.DeviceIdType.MESH,
    )


class Place:
    def __init__(self):
        self.v = lax.axis_index("var")
        self.b = lax.axis_index("band")
        self.x = self.v // 2
        self.h = self.v % 2
        self.zl = self.b // 8
        self.y = (self.b // 2) % 4
        self.core = self.b % 2
        self.right = lax.rem(self.x + 1, 4) * 2 + self.h
        self.left = lax.rem(self.x + 3, 4) * 2 + self.h
        self.over = self.x * 2 + 1 - self.h

    def band_peer(self, k):
        return lax.rem(self.b + k, NB)

    def band_source(self, k):
        return lax.rem(self.b + NB - k, NB)


def greet(me, var_peers):
    barrier = pltpu.get_barrier_semaphore()

    @pl.loop(1, NB)
    def _(k):
        pl.semaphore_signal(
            barrier, inc=1, device_id=(me.v, me.band_peer(k)), device_id_type=pl.DeviceIdType.MESH
        )

    for peer in var_peers:
        pl.semaphore_signal(
            barrier, inc=1, device_id=(peer, me.b), device_id_type=pl.DeviceIdType.MESH
        )
    return lambda: pl.semaphore_wait(barrier, NB - 1 + len(var_peers))


def rows(i, n):
    return pl.ds(pl.multiple_of(i * n, n), n)


def exchange_start(me, src, dst, send, recv):
    @pl.loop(1, NB)
    def _(k):
        d = me.band_peer(k)
        remote(src(d), dst(me.b), send.at[d], recv.at[me.b], me.v, d).start()


def exchange_wait_recv(me, src, dst, send, recv):
    @pl.loop(1, NB)
    def _(k):
        s = me.band_source(k)
        remote(src(s), dst(s), send.at[s], recv.at[s], me.v, s).wait_recv()


def exchange_wait_send(me, src, dst, send, recv):
    @pl.loop(1, NB)
    def _(k):
        d = me.band_peer(k)
        remote(src(d), dst(d), send.at[d], recv.at[d], me.v, d).wait_send()


def mix_blocks(me, transposed):
    shape = (LANES, LANES)
    token = iota(shape, 1 if transposed else 0)
    cell = iota(shape, 0 if transposed else 1)
    second = cell >= 64
    j = jnp.where(second, cell - 64, cell)
    first = (me.b + 1) // 2 - 1

    def lat(p):
        u = jnp.clip(
            ((2 * me.b + p).astype(F32) + 0.5) / 4.0 - 0.5, 0.0, 15.0
        )
        w0 = jnp.maximum(1.0 - jnp.abs(u - first.astype(F32)), 0.0)
        w1 = jnp.maximum(1.0 - jnp.abs(u - (first + 1).astype(F32)), 0.0)
        return jnp.where(second, w1, w0)

    def lon(c):
        w = (c.astype(F32) + 0.5) / 4.0 - 0.5
        d = jnp.abs(w - j.astype(F32))
        d = jnp.minimum(d, 45.0 - d)
        return jnp.where(j < 45, jnp.maximum(1.0 - d, 0.0), 0.0)

    lat0, lat1 = lat(0), lat(1)
    low = lon(token)
    end0 = jnp.where(token < 52, lat0 * lon(token + 128), 0.0)
    end1 = jnp.where(
        jnp.logical_and(token >= 52, token < 104), lat1 * lon(token + 76), 0.0
    )
    return [(m).astype(BF16) for m in (lat0 * low, lat1 * low, end0 + end1)]


def which_mix(tile):
    return tile % 2 if tile < 8 else 2


def forward_kernel(
    ids, shift, scale, fields, weight, table, places, gout,
    pre, cot, xb, posrow, slotrow,
    cols, poscol, rhi, rlo, info, got_info, slotcol, gpad, cot_out, cot_in,
    xn, sel, sel_end, perm, permb, xt, xrow, wq, part, fwd, from_left, from_right,
    zout, zin, window,
    info_s, info_r, cot_s, cot_r, xs, fwd_r, left_r, right_r, z_s, z_r,
):
    me = Place()
    wait_barrier = greet(me, (me.right, me.left, me.over))

    r8 = places[...]
    cols[...] = jnp.concatenate([r8, jnp.zeros((120, T), F32)], 0).T
    lane = iota((LANES, LANES), 1)
    lanef = lane.astype(F32)
    below = onehot(iota((LANES, LANES), 0) > lane)
    target_row = r8[0:1, :]
    to_shard = onehot(iota((NB, T), 0).astype(F32) == target_row)
    carry = jnp.zeros((1, LANES), F32)
    for i in range(T // LANES):
        sl = slice(i * LANES, (i + 1) * LANES)
        target = cols[sl, 0:1]
        hot = jnp.where(target == lanef, 1.0, 0.0)
        before = dot(below, hot.astype(BF16)) + carry
        rank = jnp.sum(hot * before, 1, keepdims=True)
        carry = carry + jnp.sum(hot, 0, keepdims=True)
        at = jnp.where(rank == lanef, 1.0, 0.0)
        rhi[sl, :] = (at * cols[sl, 1:2]).astype(BF16)
        rlo[sl, :] = (at * cols[sl, 2:3]).astype(BF16)
        pos = jnp.broadcast_to(target * PER + rank, (LANES, LANES))
        poscol[sl, :] = pos
        posrow[:, sl] = pos.T[0:8]
    slots = dot(to_shard, rhi[...]) * 32.0 + dot(to_shard, rlo[...])
    slots = jnp.where(iota((NB, LANES), 1) < USED, slots, -1.0)
    for d in range(NB):
        info[d] = jnp.broadcast_to(slots[d : d + 1], (8, LANES))

    wait_barrier()
    info_args = (me, lambda d: info.at[d], lambda s: got_info.at[s], info_s, info_r)
    exchange_start(*info_args)
    got_info[pl.ds(me.b, 1)] = info[pl.ds(me.b, 1)]

    xn[:, :, :, 1408:1536] = jnp.zeros((2, 4, 80, 128), BF16)

    @pl.loop(0, 4)
    def _(s):
        for pair in range(5):
            halves = []
            for k in (2 * pair, 2 * pair + 1):
                at = ids[k]
                halves.append((fields[s, k].astype(F32) - shift[at]) * scale[at])
            for p in range(2):
                both = jnp.concatenate([n[8 * p : 8 * p + 8] for n in halves], 0)
                xn[p, s, 16 * pair : 16 * pair + 16, 0:1440] = both.astype(BF16)

    @pl.loop(0, 8)
    def _(i):
        n = iota((LANES, E), 1)
        k = iota((LANES, E), 0) + i * LANES
        sel[rows(i, LANES), :] = onehot(k == (n & 127) * 8 + (n >> 7))

    @pl.loop(0, 4)
    def _(i):
        n = iota((LANES, E), 1)
        k = iota((LANES, E), 0) + i * LANES
        sel_end[rows(i, LANES), :] = onehot(k == ((n & 127) - 52) * 8 + (n >> 7))

    @pl.loop(0, 4)
    def _(i):
        out = pl.ds(pl.multiple_of(i * 256, 256), 256)
        low = dot(xn[...].reshape(640, T)[:, 0:1024], sel[:, out]).astype(BF16)
        end = (
            dot(xn[0].reshape(320, T)[:, 1024:1536], sel[0:512, out])
            + dot(xn[1].reshape(320, T)[:, 1024:1536], sel_end[:, out])
        ).astype(BF16)
        for q in range(2):
            at = pl.ds(pl.multiple_of((2 * i + q) * 80, 80), 80)
            lanes = slice(q * 128, q * 128 + 128)
            for s in range(4):
                for p in range(2):
                    tile = 2 * s + p
                    first = (p * 4 + s) * 80
                    xt[at, tile * 128 : tile * 128 + 128] = low[first : first + 80, lanes]
                xt[at, 1024 + s * 128 : 1152 + s * 128] = end[s * 80 : s * 80 + 80, lanes]

    eye = onehot(iota((LANES, LANES), 0) == lane)

    @pl.loop(0, T // LANES)
    def _(i):
        xrow[rows(i, LANES), :] = lax.dot_general(
            eye, xt[:, rows(i, LANES)], (((1,), (1,)), ((), ())), preferred_element_type=F32
        ).astype(BF16)

    n = iota((80, 640), 1)
    g = iota((80, 640), 0)
    for dx in range(8):
        perm[dx * 80 : dx * 80 + 80, :] = onehot(n == g * 8 + dx)

    def quarter(j, ahead):
        at = lax.rem(me.x + ahead, 4)
        wq[...] = dot(perm[...], weight[:, pl.ds(pl.multiple_of(at * 256, 256), 256)]).astype(BF16)

        @pl.loop(0, T // PIECE)
        def _(i):
            part[j, rows(i, PIECE), :] = dot(xrow[rows(i, PIECE), :], wq[...]).astype(BF16)

    def piece(ref, p):
        return ref.at[pl.ds(p * PIECE, PIECE)]

    sends = []

    def send(copy):
        copy.start()
        sends.append(copy)

    quarter(0, 2)
    for p in PIECES:
        send(remote(piece(part.at[0], p), piece(fwd, p), xs.at[p], fwd_r.at[p],
                    me.right if p < 3 else me.left, me.b))
    quarter(1, 1)
    for p in (3, 4, 5):
        send(remote(piece(part.at[1], p), piece(from_left, p), xs.at[6 + p], left_r.at[p],
                    me.right, me.b))
    quarter(2, 3)
    for p in (0, 1, 2):
        send(remote(piece(part.at[2], p), piece(from_right, p), xs.at[6 + p], right_r.at[p],
                    me.left, me.b))

    exchange_wait_recv(*info_args)
    gpad[1440:T, :] = jnp.zeros((T - 1440, LANES), BF16)
    gpad[0:1440, :] = gout[...]
    same = iota((PER, LANES), 0) == iota((PER, LANES), 1)

    @pl.loop(0, NB)
    def _(s):
        asked = jnp.broadcast_to(got_info[s][0:1], (PER, LANES))
        at = jnp.sum(jnp.where(same, asked, 0.0), 1, keepdims=True)
        slotcol[rows(s, PER), :] = jnp.broadcast_to(at, (PER, LANES))

    wide = iota((384, T), 1).astype(F32)

    @pl.loop(0, 4)
    def _(i):
        hot = onehot(slotcol[rows(i, 384), 0:1] == wide)
        cot_out[rows(i, 384), :] = dot(hot, gpad[...]).astype(BF16)

    cot_args = (
        me,
        lambda d: cot_out.at[rows(d, PER)],
        lambda s: cot_in.at[rows(s, PER)],
        cot_s,
        cot_r,
    )
    exchange_start(*cot_args)
    cot_in[rows(me.b, PER), :] = cot_out[rows(me.b, PER), :]
    for i in range(T // LANES):
        sl = slice(i * LANES, (i + 1) * LANES)
        slotrow[:, sl] = slotcol[sl, :].T[0:8]

    quarter(3, 0)

    for p in PIECES:
        if p < 3:
            remote(piece(part.at[0], p), piece(fwd, p), xs.at[p], fwd_r.at[p],
                   me.left, me.b).wait_recv()
            sl = slice(p * PIECE, (p + 1) * PIECE)
            part[1, sl, :] = (part[1, sl, :].astype(F32) + fwd[sl, :].astype(F32)).astype(BF16)
            send(remote(piece(part.at[1], p), piece(from_left, p), xs.at[12 + p], left_r.at[p],
                        me.right, me.b))
        else:
            remote(piece(part.at[0], p), piece(fwd, p), xs.at[p], fwd_r.at[p],
                   me.right, me.b).wait_recv()
            sl = slice(p * PIECE, (p + 1) * PIECE)
            part[2, sl, :] = (part[2, sl, :].astype(F32) + fwd[sl, :].astype(F32)).astype(BF16)
            send(remote(piece(part.at[2], p), piece(from_right, p), xs.at[12 + p], right_r.at[p],
                        me.left, me.b))

    r = iota((640, 1), 0)

    def steps(a, size, count):
        at = jnp.zeros_like(a)
        for i in range(1, count):
            at = at + jnp.where(a >= i * size, 1, 0)
        return at

    core = steps(r, 320, 2)
    r = r - 320 * core
    y = steps(r, 80, 4)
    r = r - 80 * y
    zl = steps(r, 20, 4)
    n = 20 * (zl * 8 + y * 2 + core) + r - 20 * zl
    permb[...] = onehot(iota((640, 640), 1) == (n & 7) * 80 + (n >> 3))

    @pl.loop(0, T // PIECE)
    def _(i):
        xb[:, rows(i, PIECE)] = dot(permb[...], xt[:, rows(i, PIECE)]).astype(BF16)

    first = (me.b + 1) // 2 - 1
    window[...] = jnp.zeros((LANES, LANES), F32)
    window[0:45, :] = table[jnp.maximum(first, 0)]
    window[64:109, :] = table[jnp.minimum(first + 1, 15)]
    position = [
        jnp.dot(m.astype(F32), window[...], precision=HI, preferred_element_type=F32)
        for m in mix_blocks(me, False)
    ]

    for p in PIECES:
        src = part.at[1]
        remote(piece(src, p), piece(from_left, p), xs.at[p], left_r.at[p], me.left, me.b).wait_recv()
        remote(piece(src, p), piece(from_right, p), xs.at[p], right_r.at[p], me.right, me.b).wait_recv()
        sl = slice(p * PIECE, (p + 1) * PIECE)
        total = (
            part[3, sl, :].astype(F32) + from_left[sl, :].astype(F32)
        ) + from_right[sl, :].astype(F32)
        mine = jnp.where(me.h == 0, total[:, 0:128], total[:, 128:256])
        other = jnp.where(me.h == 0, total[:, 128:256], total[:, 0:128])
        zout[sl, :] = other.astype(BF16)
        send(remote(piece(zout, p), piece(zin, p), z_s.at[p], z_r.at[p], me.over, me.b))
        pre[sl, :] = mine + jnp.concatenate(
            [position[which_mix(2 * p)], position[which_mix(2 * p + 1)]], 0
        )

    exchange_wait_recv(*cot_args)

    @pl.loop(0, 4)
    def _(i):
        hot = onehot(poscol[rows(i, 384), 0:1] == wide)
        cot[rows(i, 384), :] = dot(hot, cot_in[...]).astype(BF16)

    for p in PIECES:
        remote(piece(zout, p), piece(zin, p), z_s.at[p], z_r.at[p], me.over, me.b).wait_recv()
        sl = slice(p * PIECE, (p + 1) * PIECE)
        pre[sl, :] = pre[sl, :] + zin[sl, :].astype(F32)

    for copy in sends:
        copy.wait_send()
    exchange_wait_send(*info_args)
    exchange_wait_send(*cot_args)


def backward_kernel(
    pre, cot, xb, posrow, slotrow, gain_in, bias_in,
    embed, grad_weight, grad_table, grad_gain, grad_bias,
    stat, packed, got_stat, statcol, emb, emb_out, emb_in, dg,
    core_out, core_in, gw, y_out, y_in, zl_out, zl_in,
    outer, outer_in, inner, chip, chip_in, tables,
    stat_s, stat_r, emb_s, emb_r, dz_s, dz_r, dx_s, dr_r, dl_r, df_s, df_r,
    core_s, core_r, y_s, y_r, zl_s, zl_r, t_s, t_r, tab_s, tab_r,
):
    me = Place()
    var_peers = [lax.rem(me.v + k, NV) for k in range(1, NV)]
    wait_barrier = greet(me, var_peers)
    gain = gain_in[...]
    bias = bias_in[...]
    sends = []

    def send(copy):
        copy.start()
        sends.append(copy)

    lane = iota((PIECE, LANES), 1)
    for p in range(T // PIECE):
        sl = slice(p * PIECE, (p + 1) * PIECE)
        a = pre[sl, :]
        g = cot[sl, :].astype(F32) * gain
        sums = [jnp.sum(q, 1, keepdims=True) for q in (a, a * a, g, g * a)]
        base = 0 if p < 3 else 4
        block = jnp.zeros((PIECE, LANES), F32)
        for k in range(4):
            block = jnp.where(lane == base + k, sums[k], block)
        stat[sl, :] = block
    flat = stat[...].T
    packed[...] = flat[0:8, 0:HALF] + flat[0:8, HALF:T]
    wait_barrier()
    for k in range(1, NV):
        send(remote(packed, got_stat.at[me.v], stat_s.at[k - 1], stat_r.at[me.v],
                    var_peers[k - 1], me.b))
    got_stat[pl.ds(me.v, 1)] = packed[...][None]
    for k in range(1, NV):
        src = lax.rem(me.v + NV - k, NV)
        remote(packed, got_stat.at[src], stat_s.at[k - 1], stat_r.at[src], src, me.b).wait_recv()
    total = got_stat[0]
    for k in range(1, NV):
        total = total + got_stat[k]
    statcol[...] = jnp.concatenate(
        [jnp.concatenate([total, total], 1), jnp.zeros((120, T), F32)], 0
    ).T

    own = dg.at[0, me.h]
    gain_sum = jnp.zeros((1, LANES), F32)
    bias_sum = jnp.zeros((1, LANES), F32)
    for half in range(2):
        for p in range(3 * half, 3 * half + 3):
            sl = slice(p * PIECE, (p + 1) * PIECE)
            s1, s2, sg, sq = [statcol[sl, 4 * half + k : 4 * half + k + 1] for k in range(4)]
            mean = s1 / E
            inv = lax.rsqrt(s2 / E - mean * mean + EPS)
            xhat = (pre[sl, :] - mean) * inv
            up = cot[sl, :].astype(F32)
            emb[sl, :] = (xhat * gain + bias).astype(BF16)
            along = inv * (sq - mean * sg) / E
            d = inv * (up * gain - sg / E - xhat * along)
            own[sl, :] = d.astype(BF16)
            gain_sum = gain_sum + jnp.sum(up * xhat, 0, keepdims=True)
            bias_sum = bias_sum + jnp.sum(up, 0, keepdims=True)
        hs = pl.ds(half * HALF, HALF)
        send(remote(own.at[hs], own.at[hs], dz_s.at[half], dz_r.at[half], me.over, me.b))
        at = 2 * me.h + half
        send(remote(own.at[hs], dg.at[1, me.h, hs], dx_s.at[half], dr_r.at[at], me.right, me.b))
        send(remote(own.at[hs], dg.at[2, me.h, hs], dx_s.at[2 + half], dl_r.at[at], me.left, me.b))

    tall = iota((384, T), 0).astype(F32)

    @pl.loop(0, 4)
    def _(i):
        hot = onehot(posrow[0:1, :] == tall + (i * 384).astype(F32))
        emb_out[rows(i, 384), :] = dot(hot, emb[...]).astype(BF16)

    emb_args = (
        me,
        lambda d: emb_out.at[rows(d, PER)],
        lambda s: emb_in.at[rows(s, PER)],
        emb_s,
        emb_r,
    )
    exchange_start(*emb_args)
    emb_in[rows(me.b, PER), :] = emb_out[rows(me.b, PER), :]

    mixes = mix_blocks(me, True)
    rows_term = jnp.zeros((LANES, LANES), F32)
    for i in range(T // LANES):
        rows_term = rows_term + dot(mixes[which_mix(i)], own[i * LANES : (i + 1) * LANES, :])
    even = me.core == 0
    outer[...] = jnp.where(even, rows_term[0:48], rows_term[64:112])
    at = iota((48, LANES), 0)
    inner[...] = jnp.where(even, rows_term[64:112], rows_term[0:48])
    across = jnp.where(even, lax.rem(me.b + NB - 1, NB), lax.rem(me.b + 1, NB))
    mate = jnp.where(even, me.b + 1, me.b - 1)
    outer_copy = remote(outer, outer_in, t_s.at[0], t_r.at[0], me.v, across)
    send(outer_copy)

    over = dg.at[0, 1 - me.h]
    for half in range(2):
        hs = pl.ds(half * HALF, HALF)
        remote(own.at[hs], over.at[hs], dz_s.at[half], dz_r.at[half], me.over, me.b).wait_recv()
        at2 = 2 * (1 - me.h) + half
        send(remote(over.at[hs], dg.at[1, 1 - me.h, hs], dx_s.at[4 + half], dr_r.at[at2],
                    me.right, me.b))
        send(remote(over.at[hs], dg.at[2, 1 - me.h, hs], dx_s.at[6 + half], dl_r.at[at2],
                    me.left, me.b))

    outer_copy.wait_recv()
    both = inner[...] + outer_in[...]
    both = jnp.where(at == 45, gain_sum, jnp.where(at == 46, bias_sum, both))
    chip[...] = both
    chip_copy = remote(chip, chip_in, t_s.at[1], t_r.at[1], me.v, mate)
    send(chip_copy)

    mate_core = 1 - me.core

    def multiply(c):
        left = xb
        right = jnp.concatenate([dg[c, 0], dg[c, 1]], 1)
        theirs = left[pl.ds(pl.multiple_of(mate_core * 320, 320), 320), :]
        core_out[c] = dot(theirs, right).astype(BF16)
        send(remote(core_out.at[c], core_in.at[c], core_s.at[c], core_r.at[c], me.v, mate))
        mine = left[pl.ds(pl.multiple_of(me.core * 320, 320), 320), :]
        gw[c] = dot(mine, right)

    def over_y(c):
        remote(core_out.at[c], core_in.at[c], core_s.at[c], core_r.at[c], me.v, mate).wait_recv()
        y_out[c] = (gw[c] + core_in[c].astype(F32)).astype(BF16)
        for k in range(1, 4):
            to = lax.rem(me.y + k, 4)
            src = y_out.at[c, rows(to, 80)]
            send(remote(src, y_in.at[c, k - 1], y_s.at[c, k - 1], y_r.at[c, k - 1],
                        me.v, me.zl * 8 + to * 2 + me.core))

    spread_r = iota((128, 80), 0)
    spread_c = iota((128, 80), 1)
    group = spread_r >> 5
    inside = spread_r & 31
    spread = onehot(
        jnp.logical_and(inside < 20, spread_c == group * 20 + inside)
    )

    def over_z(c):
        total = y_out[c, rows(me.y, 80), :].astype(F32)
        for k in range(1, 4):
            src = lax.rem(me.y + 4 - k, 4)
            remote(y_out.at[c, rows(src, 80)], y_in.at[c, k - 1], y_s.at[c, k - 1],
                   y_r.at[c, k - 1], me.v, me.zl * 8 + src * 2 + me.core).wait_recv()
            total = total + y_in[c, k - 1].astype(F32)
        zl_out[c] = dot(spread, total.astype(BF16)).astype(BF16)
        for k in range(1, 4):
            to = lax.rem(me.zl + k, 4)
            send(remote(zl_out.at[c, rows(to, 32)], zl_in.at[c, k - 1], zl_s.at[c, k - 1],
                        zl_r.at[c, k - 1], me.v, to * 8 + me.y * 2 + me.core))

    ahead = (0, 3, 1, 2)

    def finish(c):
        total = zl_out[c, rows(me.zl, 32), :].astype(F32)
        for k in range(1, 4):
            src = lax.rem(me.zl + 4 - k, 4)
            remote(zl_out.at[c, rows(src, 32)], zl_in.at[c, k - 1], zl_s.at[c, k - 1],
                   zl_r.at[c, k - 1], me.v, src * 8 + me.y * 2 + me.core).wait_recv()
            total = total + zl_in[c, k - 1].astype(F32)
        x = lax.rem(me.x + ahead[c], 4)
        grad_weight[:, pl.ds(pl.multiple_of(x * 256, 256), 256)] = total[0:20]

    def await_x(c):
        for hh in range(2):
            for half in range(2):
                hs = pl.ds(half * HALF, HALF)
                src = dg.at[0, hh, hs]
                if c == 1:
                    remote(src, dg.at[1, hh, hs], dx_s.at[0], dr_r.at[2 * hh + half],
                           me.left, me.b).wait_recv()
                    if half == 0:
                        send(remote(dg.at[1, hh, hs], dg.at[3, hh, hs], df_s.at[2 * hh],
                                    df_r.at[2 * hh], me.right, me.b))
                elif c == 2:
                    remote(src, dg.at[2, hh, hs], dx_s.at[0], dl_r.at[2 * hh + half],
                           me.right, me.b).wait_recv()
                    if half == 1:
                        send(remote(dg.at[2, hh, hs], dg.at[3, hh, hs], df_s.at[2 * hh + 1],
                                    df_r.at[2 * hh + 1], me.left, me.b))
                else:
                    remote(src, dg.at[3, hh, hs], dx_s.at[0], df_r.at[2 * hh + half],
                           me.left, me.b).wait_recv()

    multiply(0)

    chip_copy.wait_recv()
    m = me.zl * 4 + me.y
    tables[pl.ds(m, 1)] = (chip[...] + chip_in[...])[None]
    for k in range(1, 16):
        to = lax.rem(m + k, 16)
        send(remote(tables.at[m], tables.at[m], tab_s.at[k - 1], tab_r.at[m],
                    me.v, to * 2 + me.core))

    await_x(1)
    await_x(2)
    multiply(1)
    over_y(0)
    multiply(2)
    over_y(1)
    over_z(0)

    exchange_wait_recv(*emb_args)

    @pl.loop(0, 3)
    def _(i):
        hot = onehot(slotrow[0:1, :] == iota((480, T), 0).astype(F32) + (i * 480).astype(F32))
        embed[rows(i, 480), :] = dot(hot, emb_in[...]).astype(BF16)

    over_y(2)
    over_z(1)
    await_x(3)
    multiply(3)
    over_z(2)
    finish(0)
    over_y(3)
    finish(1)

    for k in range(1, 16):
        src = lax.rem(m + 16 - k, 16)
        remote(tables.at[src], tables.at[src], tab_s.at[k - 1], tab_r.at[src],
               me.v, src * 2 + me.core).wait_recv()
    gain_total = jnp.zeros((1, LANES), F32)
    bias_total = jnp.zeros((1, LANES), F32)
    for i in range(16):
        grad_table[i] = tables[i, 0:45, :]
        gain_total = gain_total + tables[i, 45:46, :]
        bias_total = bias_total + tables[i, 46:47, :]
    grad_gain[...] = gain_total
    grad_bias[...] = bias_total

    over_z(3)
    finish(2)
    finish(3)
    for copy in sends:
        copy.wait_send()
    exchange_wait_send(*emb_args)


def dma(*shape):
    return pltpu.SemaphoreType.DMA(shape)


def vmem(shape, dtype=BF16):
    return pltpu.VMEM(shape, dtype)


def on_device(
    fields, var_ids, var_shift, var_scale, patch_weight, pos_table,
    layer_norm_gain, layer_norm_bias, order, grad_out,
):
    token = order.reshape(8, 180)
    target = token // 1440
    slot = token % 1440
    three = jnp.stack([target, slot // 32, slot % 32], 0).astype(F32)
    ends = jnp.pad(
        three[:, :, 128:].reshape(3, 4, 104), ((0, 0), (0, 0), (0, 24)), constant_values=99.0
    )
    places = jnp.concatenate([three[:, :, :128].reshape(3, 1024), ends.reshape(3, 512)], 1)
    places = jnp.pad(places, ((0, 5), (0, 0)))

    here = pl.BlockSpec(memory_space=pltpu.VMEM)
    scalars = pl.BlockSpec(memory_space=pltpu.SMEM)
    params = functools.partial(
        pltpu.CompilerParams, has_side_effects=True, vmem_limit_bytes=56 * 1024 * 1024
    )
    shape = jax.ShapeDtypeStruct
    pre, cot, xb, posrow, slotrow = pl.pallas_call(
        forward_kernel,
        out_shape=(
            shape((T, LANES), F32),
            shape((T, LANES), BF16),
            shape((640, T), BF16),
            shape((8, T), F32),
            shape((8, T), F32),
        ),
        in_specs=[scalars] * 3 + [here] * 5,
        out_specs=(here,) * 5,
        scratch_shapes=[
            vmem((T, LANES), F32), vmem((T, LANES), F32), vmem((T, LANES)), vmem((T, LANES)),
            vmem((NB, 8, LANES), F32), vmem((NB, 8, LANES), F32), vmem((T, LANES), F32),
            vmem((T, LANES)), vmem((T, LANES)), vmem((T, LANES)),
            vmem((2, 4, 80, T)), vmem((E, E)), vmem((512, E)),
            vmem((640, 640)), vmem((640, 640)), vmem((640, T)), vmem((T, 640)),
            vmem((640, 256)), vmem((4, T, 256)), vmem((T, 256)), vmem((T, 256)), vmem((T, 256)),
            vmem((T, LANES)), vmem((T, LANES)), vmem((LANES, LANES), F32),
            dma(NB), dma(NB), dma(NB), dma(NB), dma(18), dma(6), dma(6), dma(6), dma(6), dma(6),
        ],
        compiler_params=params(collective_id=0),
        name="forward",
    )(
        var_ids, var_shift, var_scale, fields, patch_weight.reshape(640, E), pos_table,
        places, grad_out,
    )
    embed, grad_weight, grad_table, grad_gain, grad_bias = pl.pallas_call(
        backward_kernel,
        out_shape=(
            shape((1440, LANES), BF16),
            shape((20, E), F32),
            shape((16, 45, LANES), F32),
            shape((1, LANES), F32),
            shape((1, LANES), F32),
        ),
        in_specs=[here] * 7,
        out_specs=(here,) * 5,
        scratch_shapes=[
            vmem((T, LANES), F32), vmem((8, HALF), F32), vmem((NV, 8, HALF), F32),
            vmem((T, LANES), F32), vmem((T, LANES)), vmem((T, LANES)), vmem((T, LANES)),
            vmem((4, 2, T, LANES)),
            vmem((4, 320, 256)), vmem((4, 320, 256)), vmem((4, 320, 256), F32),
            vmem((4, 320, 256)), vmem((4, 3, 80, 256)),
            vmem((4, 128, 256)), vmem((4, 3, 32, 256)),
            vmem((48, LANES), F32), vmem((48, LANES), F32), vmem((48, LANES), F32),
            vmem((48, LANES), F32), vmem((48, LANES), F32), vmem((16, 48, LANES), F32),
            dma(7), dma(8), dma(NB), dma(NB), dma(2), dma(2), dma(8), dma(4), dma(4),
            dma(4), dma(4), dma(4), dma(4), dma(4, 3), dma(4, 3), dma(4, 3), dma(4, 3),
            dma(2), dma(2), dma(15), dma(16),
        ],
        compiler_params=params(collective_id=1),
        name="backward",
    )(
        pre, cot, xb, posrow, slotrow,
        layer_norm_gain.reshape(1, LANES), layer_norm_bias.reshape(1, LANES),
    )
    return embed, grad_weight, grad_table, grad_gain.reshape(LANES), grad_bias.reshape(LANES)


def solution(mesh):
    in_specs = (
        P(None, "var", "band", None),
        P("var"),
        P(),
        P(),
        P("var", None, None),
        P(None, None, "var"),
        P("var"),
        P("var"),
        P("band"),
        P("band", "var"),
    )
    out_specs = (
        P("band", "var"),
        P(("var", "band"), None),
        P(None, None, "var"),
        P("var"),
        P("var"),
    )
    return jax.shard_map(
        on_device, mesh=mesh, in_specs=in_specs, out_specs=out_specs, check_vma=False
    )
```

```python
import functools

import jax
import jax.numpy as jnp
from jax import lax
from jax.experimental import pallas as pl
from jax.experimental.pallas import tpu as pltpu
from jax.sharding import PartitionSpec as P

EPS = 1e-05
T = 1536
LANES = 128
NB = 32
NV = 8
PER = 48
USED = 45
E = 1024
PIECE = 384
SENT = 368
F32 = jnp.float32
BF16 = jnp.bfloat16
HI = lax.Precision.HIGHEST


def iota(shape, dim):
    return lax.broadcasted_iota(jnp.int32, shape, dim)


def onehot(cond):
    return jnp.where(cond, 1.0, 0.0).astype(BF16)


def dot(a, b):
    return jnp.dot(a, b, preferred_element_type=F32)


def remote(src, dst, send, recv, v, b):
    return pltpu.make_async_remote_copy(
        src_ref=src,
        dst_ref=dst,
        send_sem=send,
        recv_sem=recv,
        device_id=(v, b),
        device_id_type=pl.DeviceIdType.MESH,
    )


class Place:
    def __init__(self):
        self.v = lax.axis_index("var")
        self.b = lax.axis_index("band")
        self.x = self.v // 2
        self.h = self.v % 2
        self.zl = self.b // 8
        self.y = (self.b // 2) % 4
        self.core = self.b % 2
        self.right = lax.rem(self.x + 1, 4) * 2 + self.h
        self.left = lax.rem(self.x + 3, 4) * 2 + self.h
        self.over = self.x * 2 + 1 - self.h

    def band_peer(self, k):
        return lax.rem(self.b + k, NB)

    def band_source(self, k):
        return lax.rem(self.b + NB - k, NB)


def greet(me, var_peers):
    barrier = pltpu.get_barrier_semaphore()

    @pl.loop(1, NB)
    def _(k):
        pl.semaphore_signal(
            barrier, inc=1, device_id=(me.v, me.band_peer(k)), device_id_type=pl.DeviceIdType.MESH
        )

    for peer in var_peers:
        pl.semaphore_signal(
            barrier, inc=1, device_id=(peer, me.b), device_id_type=pl.DeviceIdType.MESH
        )
    return lambda: pl.semaphore_wait(barrier, NB - 1 + len(var_peers))


def rows(i, n):
    return pl.ds(pl.multiple_of(i * n, n), n)


def exchange_start(me, src, dst, send, recv):
    @pl.loop(1, NB)
    def _(k):
        d = me.band_peer(k)
        remote(src(d), dst(me.b), send.at[d], recv.at[me.b], me.v, d).start()


def exchange_wait_recv(me, src, dst, send, recv):
    @pl.loop(1, NB)
    def _(k):
        s = me.band_source(k)
        remote(src(s), dst(s), send.at[s], recv.at[s], me.v, s).wait_recv()


def exchange_wait_send(me, src, dst, send, recv):
    @pl.loop(1, NB)
    def _(k):
        d = me.band_peer(k)
        remote(src(d), dst(d), send.at[d], recv.at[d], me.v, d).wait_send()


def mix_blocks(me, transposed):
    shape = (LANES, LANES)
    token = iota(shape, 1 if transposed else 0)
    cell = iota(shape, 0 if transposed else 1)
    second = cell >= 64
    j = jnp.where(second, cell - 64, cell)
    first = (me.b + 1) // 2 - 1

    def lat(p):
        u = jnp.clip(
            ((2 * me.b + p).astype(F32) + 0.5) / 4.0 - 0.5, 0.0, 15.0
        )
        w0 = jnp.maximum(1.0 - jnp.abs(u - first.astype(F32)), 0.0)
        w1 = jnp.maximum(1.0 - jnp.abs(u - (first + 1).astype(F32)), 0.0)
        return jnp.where(second, w1, w0)

    def lon(c):
        w = (c.astype(F32) + 0.5) / 4.0 - 0.5
        d = jnp.abs(w - j.astype(F32))
        d = jnp.minimum(d, 45.0 - d)
        return jnp.where(j < 45, jnp.maximum(1.0 - d, 0.0), 0.0)

    lat0, lat1 = lat(0), lat(1)
    low = lon(token)
    end0 = jnp.where(token < 52, lat0 * lon(token + 128), 0.0)
    end1 = jnp.where(
        jnp.logical_and(token >= 52, token < 104), lat1 * lon(token + 76), 0.0
    )
    return [(m).astype(BF16) for m in (lat0 * low, lat1 * low, end0 + end1)]


def nt(a, b):
    return lax.dot_general(a, b, (((1,), (1,)), ((), ())), preferred_element_type=F32)


def sample(s):
    return pl.ds(s * PIECE, PIECE)


def sent(s):
    return pl.ds(s * PIECE, SENT)


def encoder_kernel(
    ids, shift, scale, fields_at, weight_at, table, order, gout, gain_in, bias_in,
    embed, grad_weight, grad_table, grad_gain, grad_bias,
    fields, weight, info, got_info, slotcol, posrow, poscol, slotrow, gpad, cot_out, cot_in, cot,
    xn, sel, sel_end, perm, permb, xt, xb, xrow, wq, part, leg, from_left, from_right,
    zout, zin, window, pre,
    stat, packed, stat_x, packed_z, stat_z, statcol, emb, emb_out, emb_in, dg,
    core_out, core_in, gw, y_out, y_in, zl_out, zl_in,
    outer, outer_in, inner, chip, chip_in, tables,
    load_s, info_s, info_r, cot_s, cot_r, leg_s, leg_r, dir_s, comb_s, left_r, right_r, z_s, z_r,
    sx_s, sx_r, sz_s, sz_r, emb_s, emb_r, dz_s, dz_r, dx_s, dr_r, dl_r, df_s, df_r,
    core_s, core_r, y_s, y_r, zl_s, zl_r, t_s, t_r, tz_s, tz_r, ty_s, ty_r,
):
    me = Place()
    x_peers = [lax.rem(me.x + k, 4) * 2 + me.h for k in range(1, 4)]
    wait_barrier = greet(me, x_peers + [me.over])
    gain = gain_in[...]
    bias = bias_in[...]
    sends = []

    def send(copy):
        copy.start()
        sends.append(copy)

    loads = [pltpu.make_async_copy(weight_at, weight, load_s.at[4])]
    for s in range(4):
        loads.append(pltpu.make_async_copy(fields_at.at[s], fields.at[s], load_s.at[s]))
    for copy in loads:
        copy.start()

    o = order[...].astype(F32)
    pieces = []
    for s in range(4):
        at = 360 * s
        pieces += [o[:, at : at + 128], o[:, at + 180 : at + 308]]
        pieces.append(
            jnp.concatenate(
                [o[:, at + 128 : at + 180], o[:, at + 308 : at + 360],
                 jnp.full((1, 24), 99.0 * 1440.0, F32)], 1
            )
        )
    o = jnp.concatenate(pieces, 1)
    target = jnp.floor((o + 0.5) * (1.0 / 1440.0))
    slot = o - target * 1440.0
    high = jnp.floor(slot * (1.0 / 32.0))
    low = slot - high * 32.0
    to_shard = jnp.where(iota((NB, T), 0).astype(F32) == target, 1.0, 0.0)
    tiles = [to_shard[:, i * 128 : i * 128 + 128] for i in range(12)]
    lane = iota((LANES, LANES), 1)
    above = onehot(iota((LANES, LANES), 0) < lane)
    before = dot(jnp.concatenate(tiles, 0).astype(BF16), above)
    carry = jnp.zeros((NB, 1), F32)
    ranks = []
    for i in range(12):
        ranks.append(
            jnp.sum(tiles[i] * (before[i * NB : i * NB + NB] + carry), 0, keepdims=True)
        )
        carry = carry + jnp.sum(tiles[i], 1, keepdims=True)
    rank = jnp.concatenate(ranks, 1)
    posrow[...] = jnp.broadcast_to(target * PER + rank, (8, T))
    at = iota((LANES, T), 0).astype(F32) == rank
    shards = to_shard.astype(BF16)
    slots = nt(shards, jnp.where(at, high, 0.0).astype(BF16)) * 32.0 + nt(
        shards, jnp.where(at, low, 0.0).astype(BF16)
    )
    slots = jnp.where(iota((NB, LANES), 1) < USED, slots, -1.0)
    for d in range(NB):
        info[d] = jnp.broadcast_to(slots[d : d + 1], (8, LANES))
    wait_barrier()
    info_args = (me, lambda d: info.at[d], lambda s: got_info.at[s], info_s, info_r)
    exchange_start(*info_args)
    got_info[pl.ds(me.b, 1)] = info[pl.ds(me.b, 1)]

    xn[:, :, :, 1408:1536] = jnp.zeros((2, 4, 80, 128), BF16)
    for s in range(4):
        pad = slice(s * PIECE + SENT, (s + 1) * PIECE)
        zero = jnp.zeros((PIECE - SENT, 256), BF16)
        from_left[pad, :] = zero
        from_right[pad, :] = zero
        zin[pad, :] = zero[:, 0:128]
        for c in range(4):
            for hh in range(2):
                dg[c, hh, pad, :] = zero[:, 0:128]

    @pl.loop(0, 8)
    def _(i):
        n = iota((LANES, E), 1)
        k = iota((LANES, E), 0) + i * LANES
        sel[rows(i, LANES), :] = onehot(k == (n & 127) * 8 + (n >> 7))

    @pl.loop(0, 4)
    def _(i):
        n = iota((LANES, E), 1)
        k = iota((LANES, E), 0) + i * LANES
        sel_end[rows(i, LANES), :] = onehot(k == ((n & 127) - 52) * 8 + (n >> 7))

    n = iota((80, 640), 1)
    g = iota((80, 640), 0)
    for dx in range(8):
        perm[dx * 80 : dx * 80 + 80, :] = onehot(n == g * 8 + dx)
    loads[0].wait()
    for i in range(4):
        lanes = slice(i * 256, i * 256 + 256)
        wq[:, lanes] = dot(perm[...], weight[:, lanes]).astype(BF16)
    eye = onehot(iota((PIECE, PIECE), 0) == iota((PIECE, PIECE), 1))

    def patches(ch):
        for s in (2 * ch, 2 * ch + 1):
            loads[1 + s].wait()

            @pl.loop(0, 5)
            def _(pair):
                halves = []
                for j in range(2):
                    k = 2 * pair + j
                    at = ids[k]
                    halves.append((fields[s, k].astype(F32) - shift[at]) * scale[at])
                for p in range(2):
                    both = jnp.concatenate([q[8 * p : 8 * p + 8] for q in halves], 0)
                    xn[p, s, rows(pair, 16), 0:1440] = both.astype(BF16)

        x = [xn[p, 2 * ch : 2 * ch + 2].reshape(160, T) for p in range(2)]
        both = jnp.concatenate(x, 0)
        for i in range(4):
            out = slice(i * 256, i * 256 + 256)
            low = dot(both[:, 0:1024], sel[:, out]).astype(BF16)
            end = (
                dot(x[0][:, 1024:1536], sel[0:512, out])
                + dot(x[1][:, 1024:1536], sel_end[:, out])
            ).astype(BF16)
            for q in range(2):
                at = slice((2 * i + q) * 80, (2 * i + q) * 80 + 80)
                lanes = slice(q * 128, q * 128 + 128)
                for s in range(2):
                    base = (2 * ch + s) * PIECE
                    for p in range(2):
                        first = (2 * p + s) * 80
                        xt[at, base + p * 128 : base + p * 128 + 128] = low[
                            first : first + 80, lanes
                        ]
                    xt[at, base + 256 : base + 384] = end[s * 80 : s * 80 + 80, lanes]

    def partials(s):
        xrow[...] = nt(eye, xt[:, sample(s)]).astype(BF16)
        for j, ahead in ((0, 2), (1, 1), (2, 3), (3, 0)):
            at = lax.rem(me.x + ahead, 4)
            lanes = pl.ds(pl.multiple_of(at * 256, 256), 256)
            part[j, sample(s), :] = dot(xrow[...], wq[:, lanes]).astype(BF16)

    def onward(s):
        return (me.right, me.left) if s % 2 == 0 else (me.left, me.right)

    def start_x(s):
        ahead, back = onward(s)
        send(remote(part.at[0, sent(s)], leg.at[sent(s)], leg_s.at[s], leg_r.at[s], ahead, me.b))
        if s % 2 == 0:
            send(remote(part.at[2, sent(s)], from_right.at[sent(s)], dir_s.at[s], right_r.at[s],
                        back, me.b))
        else:
            send(remote(part.at[1, sent(s)], from_left.at[sent(s)], dir_s.at[s], left_r.at[s],
                        back, me.b))

    def pass_on(s):
        ahead, back = onward(s)
        remote(part.at[0, sent(s)], leg.at[sent(s)], leg_s.at[s], leg_r.at[s],
               back, me.b).wait_recv()
        j = 1 if s % 2 == 0 else 2
        at = sent(s)
        part[j, at, :] = (part[j, at, :].astype(F32) + leg[at, :].astype(F32)).astype(BF16)
        into, sem = (from_left, left_r) if s % 2 == 0 else (from_right, right_r)
        send(remote(part.at[j, at], into.at[at], comb_s.at[s], sem.at[s], ahead, me.b))

    def finish_x(s):
        src = part.at[0, sent(s)]
        remote(src, from_left.at[sent(s)], dir_s.at[s], left_r.at[s], me.left, me.b).wait_recv()
        remote(src, from_right.at[sent(s)], dir_s.at[s], right_r.at[s], me.right, me.b).wait_recv()
        sl = sample(s)
        total = (
            part[3, sl, :].astype(F32) + from_left[sl, :].astype(F32)
        ) + from_right[sl, :].astype(F32)
        mine = jnp.where(me.h == 0, total[:, 0:128], total[:, 128:256])
        other = jnp.where(me.h == 0, total[:, 128:256], total[:, 0:128])
        zout[sl, :] = other.astype(BF16)
        send(remote(zout.at[sent(s)], zin.at[sent(s)], z_s.at[s], z_r.at[s], me.over, me.b))
        pre[sl, :] = mine

    def finish_z(s):
        remote(zout.at[sent(s)], zin.at[sent(s)], z_s.at[s], z_r.at[s], me.over, me.b).wait_recv()
        sl = sample(s)
        pre[sl, :] = pre[sl, :] + zin[sl, :].astype(F32) + jnp.concatenate(position, 0)

    cot_args = (
        me,
        lambda d: cot_out.at[rows(d, PER)],
        lambda s: cot_in.at[rows(s, PER)],
        cot_s,
        cot_r,
    )
    wide = iota((384, T), 1).astype(F32)

    def answer():
        gpad[1440:T, :] = jnp.zeros((T - 1440, LANES), BF16)
        gpad[0:1440, :] = gout[...]
        exchange_wait_recv(*info_args)
        asked = jnp.concatenate([got_info[s][0:1] for s in range(NB)], 0)
        asked = jnp.concatenate([asked, jnp.zeros((LANES - NB, LANES), F32)], 0).T
        for i in range(4):
            at = jnp.concatenate([asked[0:PER, s : s + 1] for s in range(8 * i, 8 * i + 8)], 0)
            slotcol[i * 384 : i * 384 + 384, :] = jnp.broadcast_to(at, (384, LANES))
            cot_out[i * 384 : i * 384 + 384, :] = dot(onehot(at == wide), gpad[...]).astype(BF16)
        exchange_start(*cot_args)
        cot_in[rows(me.b, PER), :] = cot_out[rows(me.b, PER), :]

    def place_cot():
        exchange_wait_recv(*cot_args)
        for i in range(4):
            sl = slice(i * 384, i * 384 + 384)
            cot[sl, :] = dot(onehot(poscol[sl, 0:1] == wide), cot_in[...]).astype(BF16)

    def local_sums(ch):
        lane = iota((PIECE, LANES), 1)
        for j in range(2):
            sl = sample(2 * ch + j)
            a = pre[sl, :]
            g = cot[sl, :].astype(F32) * gain
            block = jnp.zeros((PIECE, LANES), F32)
            for k, q in enumerate((a, a * a, g, g * a)):
                block = jnp.where(lane == 4 * j + k, jnp.sum(q, 1, keepdims=True), block)
            stat[sl, :] = block
        flat = stat[pl.ds(ch * 768, 768), :].T
        packed[ch] = flat[0:8, 0:PIECE] + flat[0:8, PIECE : 2 * PIECE]
        stat_x[ch, pl.ds(me.x, 1)] = packed[ch][None]
        for k in range(1, 4):
            send(remote(packed.at[ch], stat_x.at[ch, me.x], sx_s.at[ch, k - 1],
                        sx_r.at[ch, me.x], x_peers[k - 1], me.b))

    def sums_x(ch):
        for k in range(1, 4):
            src = lax.rem(me.x + 4 - k, 4)
            remote(packed.at[ch], stat_x.at[ch, src], sx_s.at[ch, k - 1], sx_r.at[ch, src],
                   src * 2 + me.h, me.b).wait_recv()
        packed_z[ch] = (stat_x[ch, 0] + stat_x[ch, 1]) + (stat_x[ch, 2] + stat_x[ch, 3])
        send(remote(packed_z.at[ch], stat_z.at[ch], sz_s.at[ch], sz_r.at[ch], me.over, me.b))

    def sums_z(ch):
        remote(packed_z.at[ch], stat_z.at[ch], sz_s.at[ch], sz_r.at[ch], me.over, me.b).wait_recv()
        total = packed_z[ch] + stat_z[ch]
        statcol[ch] = jnp.concatenate([total, jnp.zeros((120, PIECE), F32)], 0).T

    own = dg.at[0, me.h]
    over = dg.at[0, 1 - me.h]
    totals = [jnp.zeros((1, LANES), F32), jnp.zeros((1, LANES), F32)]

    def send_x(block, hh, s):
        k = 1 if s % 2 == 0 else 0
        at = sent(s)
        two = [
            remote(block.at[at], dg.at[1, hh, at], dx_s.at[hh, s, 0], dr_r.at[hh, s],
                   me.right, me.b),
            remote(block.at[at], dg.at[2, hh, at], dx_s.at[hh, s, 1], dl_r.at[hh, s],
                   me.left, me.b),
        ]
        send(two[1 - k])
        send(two[k])

    def norm(ch):
        for j in range(2):
            s = 2 * ch + j
            sl = sample(s)
            s1, s2, sg, sq = [statcol[ch, :, 4 * j + k : 4 * j + k + 1] for k in range(4)]
            mean = s1 / E
            inv = lax.rsqrt(s2 / E - mean * mean + EPS)
            xhat = (pre[sl, :] - mean) * inv
            up = cot[sl, :].astype(F32)
            along = inv * (sq - mean * sg) / E
            d = inv * (up * gain - sg / E - xhat * along)
            own[sl, :] = d.astype(BF16)
            send(remote(own.at[sent(s)], own.at[sent(s)], dz_s.at[s], dz_r.at[s], me.over, me.b))
            send_x(own, me.h, s)
            emb[sl, :] = (xhat * gain + bias).astype(BF16)
            totals[0] = totals[0] + jnp.sum(up * xhat, 0, keepdims=True)
            totals[1] = totals[1] + jnp.sum(up, 0, keepdims=True)

    def over_arrives(s):
        remote(own.at[sent(s)], over.at[sent(s)], dz_s.at[s], dz_r.at[s], me.over, me.b).wait_recv()
        send_x(over, 1 - me.h, s)

    def pass_d(hh, s):
        at = sent(s)
        src = dg.at[0, hh, at]
        if s % 2 == 0:
            remote(src, dg.at[1, hh, at], dx_s.at[hh, s, 0], dr_r.at[hh, s],
                   me.left, me.b).wait_recv()
            send(remote(dg.at[1, hh, at], dg.at[3, hh, at], df_s.at[hh, s], df_r.at[hh, s],
                        me.right, me.b))
        else:
            remote(src, dg.at[2, hh, at], dx_s.at[hh, s, 1], dl_r.at[hh, s],
                   me.right, me.b).wait_recv()
            send(remote(dg.at[2, hh, at], dg.at[3, hh, at], df_s.at[hh, s], df_r.at[hh, s],
                        me.left, me.b))

    def await_d(c):
        for hh in range(2):
            for s in range(4):
                at = sent(s)
                src = dg.at[0, hh, at]
                if c == 1 and s % 2 == 1:
                    remote(src, dg.at[1, hh, at], dx_s.at[hh, s, 0], dr_r.at[hh, s],
                           me.left, me.b).wait_recv()
                if c == 2 and s % 2 == 0:
                    remote(src, dg.at[2, hh, at], dx_s.at[hh, s, 1], dl_r.at[hh, s],
                           me.right, me.b).wait_recv()
                if c == 3:
                    remote(src, dg.at[3, hh, at], df_s.at[hh, s], df_r.at[hh, s],
                           me.left, me.b).wait_recv()

    tall = iota((384, T), 0).astype(F32)
    emb_args = (
        me,
        lambda d: emb_out.at[rows(d, PER)],
        lambda s: emb_in.at[rows(s, PER)],
        emb_s,
        emb_r,
    )

    def pick_emb():
        for i in range(4):
            hot = onehot(posrow[0:1, :] == tall + i * 384.0)
            emb_out[i * 384 : i * 384 + 384, :] = dot(hot, emb[...]).astype(BF16)

    def start_emb():
        exchange_start(*emb_args)
        emb_in[rows(me.b, PER), :] = emb_out[rows(me.b, PER), :]

    def place_emb():
        exchange_wait_recv(*emb_args)
        for i in range(3):
            hot = onehot(slotrow[0:1, :] == iota((480, T), 0).astype(F32) + i * 480.0)
            embed[i * 480 : i * 480 + 480, :] = dot(hot, emb_in[...]).astype(BF16)

    even = me.core == 0
    across = jnp.where(even, lax.rem(me.b + NB - 1, NB), lax.rem(me.b + 1, NB))
    mate = jnp.where(even, me.b + 1, me.b - 1)
    outer_copy = remote(outer, outer_in, t_s.at[0], t_r.at[0], me.v, across)
    chip_copy = remote(chip, chip_in, t_s.at[1], t_r.at[1], me.v, mate)

    def table_rows():
        mixes = mix_blocks(me, True)
        term = jnp.zeros((LANES, LANES), F32)
        for i in range(12):
            term = term + dot(mixes[i % 3], own[i * LANES : (i + 1) * LANES, :])
        outer[...] = jnp.where(even, term[0:48], term[64:112])
        inner[...] = jnp.where(even, term[64:112], term[0:48])
        send(outer_copy)

    def table_chip():
        outer_copy.wait_recv()
        at = iota((48, LANES), 0)
        both = inner[...] + outer_in[...]
        chip[...] = jnp.where(at == 45, totals[0], jnp.where(at == 46, totals[1], both))
        send(chip_copy)

    def table_z():
        chip_copy.wait_recv()
        tables[pl.ds(me.y, 1), pl.ds(me.zl, 1)] = (chip[...] + chip_in[...])[None, None]
        for k in range(1, 4):
            to = lax.rem(me.zl + k, 4)
            here = tables.at[me.y, me.zl]
            send(remote(here, here, tz_s.at[k - 1], tz_r.at[k - 1],
                        me.v, to * 8 + me.y * 2 + me.core))

    def table_y():
        for k in range(1, 4):
            src = lax.rem(me.zl + 4 - k, 4)
            there = tables.at[me.y, src]
            remote(there, there, tz_s.at[k - 1], tz_r.at[k - 1],
                   me.v, src * 8 + me.y * 2 + me.core).wait_recv()
        for k in range(1, 4):
            to = lax.rem(me.y + k, 4)
            here = tables.at[me.y]
            send(remote(here, here, ty_s.at[k - 1], ty_r.at[k - 1],
                        me.v, me.zl * 8 + to * 2 + me.core))

    def table_end():
        for k in range(1, 4):
            src = lax.rem(me.y + 4 - k, 4)
            there = tables.at[src]
            remote(there, there, ty_s.at[k - 1], ty_r.at[k - 1],
                   me.v, me.zl * 8 + src * 2 + me.core).wait_recv()
        gain_total = jnp.zeros((1, LANES), F32)
        bias_total = jnp.zeros((1, LANES), F32)
        for i in range(16):
            block = tables[i % 4, i // 4]
            grad_table[:, i, :] = block[0:45]
            gain_total = gain_total + block[45:46]
            bias_total = bias_total + block[46:47]
        grad_gain[...] = gain_total
        grad_bias[...] = bias_total

    mate_core = 1 - me.core

    def multiply(c):
        right = jnp.concatenate([dg[c, 0], dg[c, 1]], 1)
        theirs = xb[pl.ds(pl.multiple_of(mate_core * 320, 320), 320), :]
        core_out[c] = dot(theirs, right).astype(BF16)
        send(remote(core_out.at[c], core_in.at[c], core_s.at[c], core_r.at[c], me.v, mate))
        mine = xb[pl.ds(pl.multiple_of(me.core * 320, 320), 320), :]
        gw[c] = dot(mine, right)

    def over_y(c):
        remote(core_out.at[c], core_in.at[c], core_s.at[c], core_r.at[c], me.v, mate).wait_recv()
        y_out[c] = (gw[c] + core_in[c].astype(F32)).astype(BF16)
        for k in range(1, 4):
            to = lax.rem(me.y + k, 4)
            src = y_out.at[c, rows(to, 80)]
            send(remote(src, y_in.at[c, k - 1], y_s.at[c, k - 1], y_r.at[c, k - 1],
                        me.v, me.zl * 8 + to * 2 + me.core))

    spread_r = iota((128, 80), 0)
    spread_c = iota((128, 80), 1)
    inside = spread_r & 31
    spread = onehot(
        jnp.logical_and(inside < 20, spread_c == (spread_r >> 5) * 20 + inside)
    )

    def over_z(c):
        total = y_out[c, rows(me.y, 80), :].astype(F32)
        for k in range(1, 4):
            src = lax.rem(me.y + 4 - k, 4)
            remote(y_out.at[c, rows(src, 80)], y_in.at[c, k - 1], y_s.at[c, k - 1],
                   y_r.at[c, k - 1], me.v, me.zl * 8 + src * 2 + me.core).wait_recv()
            total = total + y_in[c, k - 1].astype(F32)
        zl_out[c] = dot(spread, total.astype(BF16)).astype(BF16)
        for k in range(1, 4):
            to = lax.rem(me.zl + k, 4)
            send(remote(zl_out.at[c, rows(to, 32)], zl_in.at[c, k - 1], zl_s.at[c, k - 1],
                        zl_r.at[c, k - 1], me.v, to * 8 + me.y * 2 + me.core))

    def finish(c):
        total = zl_out[c, rows(me.zl, 32), :].astype(F32)
        for k in range(1, 4):
            src = lax.rem(me.zl + 4 - k, 4)
            remote(zl_out.at[c, rows(src, 32)], zl_in.at[c, k - 1], zl_s.at[c, k - 1],
                   zl_r.at[c, k - 1], me.v, src * 8 + me.y * 2 + me.core).wait_recv()
            total = total + zl_in[c, k - 1].astype(F32)
        x = lax.rem(me.x + (0, 3, 1, 2)[c], 4)
        grad_weight[:, pl.ds(pl.multiple_of(x * 256, 256), 256)] = total[0:20]

    patches(0)
    partials(0)
    start_x(0)
    partials(1)
    start_x(1)
    answer()
    patches(1)
    pass_on(0)
    pass_on(1)
    partials(2)
    start_x(2)
    partials(3)
    start_x(3)

    first = (me.b + 1) // 2 - 1
    window[...] = jnp.zeros((LANES, LANES), F32)
    level = iota((45, 16, LANES), 1)
    all_rows = table[...]
    window[0:45, :] = jnp.sum(jnp.where(level == first, all_rows, 0.0), 1)
    window[64:109, :] = jnp.sum(jnp.where(level == first + 1, all_rows, 0.0), 1)
    position = [
        jnp.dot(m.astype(F32), window[...], precision=HI, preferred_element_type=F32)
        for m in mix_blocks(me, False)
    ]
    poscol[...] = jnp.concatenate([posrow[...], jnp.zeros((120, T), F32)], 0).T

    finish_x(0)
    finish_x(1)

    r = iota((640, 1), 0)

    def steps(a, size, count):
        at = jnp.zeros_like(a)
        for i in range(1, count):
            at = at + jnp.where(a >= i * size, 1, 0)
        return at

    core = steps(r, 320, 2)
    r = r - 320 * core
    y = steps(r, 80, 4)
    r = r - 80 * y
    zl = steps(r, 20, 4)
    n = 20 * (zl * 8 + y * 2 + core) + r - 20 * zl
    permb[...] = onehot(iota((640, 640), 1) == (n & 7) * 80 + (n >> 3))

    @pl.loop(0, 6)
    def _(i):
        xb[:, rows(i, 256)] = dot(permb[...], xt[:, rows(i, 256)]).astype(BF16)

    pass_on(2)
    pass_on(3)
    place_cot()
    for i in range(12):
        sl = slice(i * LANES, (i + 1) * LANES)
        slotrow[:, sl] = slotcol[sl, :].T[0:8]
    finish_z(0)
    finish_z(1)
    local_sums(0)
    finish_x(2)
    finish_x(3)
    sums_x(0)
    sums_z(0)
    norm(0)
    finish_z(2)
    finish_z(3)
    local_sums(1)
    over_arrives(0)
    over_arrives(1)
    sums_x(1)
    pass_d(me.h, 0)
    pass_d(me.h, 1)
    sums_z(1)
    norm(1)
    pass_d(1 - me.h, 0)
    pass_d(1 - me.h, 1)
    pick_emb()
    table_rows()
    over_arrives(2)
    over_arrives(3)
    start_emb()
    pass_d(me.h, 2)
    pass_d(me.h, 3)
    multiply(0)
    table_chip()
    over_y(0)
    table_z()
    pass_d(1 - me.h, 2)
    pass_d(1 - me.h, 3)
    await_d(1)
    multiply(1)
    over_z(0)
    over_y(1)
    table_y()
    await_d(2)
    multiply(2)
    over_z(1)
    over_y(2)
    place_emb()
    finish(0)
    over_z(2)
    await_d(3)
    multiply(3)
    finish(1)
    over_y(3)
    finish(2)
    table_end()
    over_z(3)
    finish(3)
    for copy in sends:
        copy.wait_send()
    exchange_wait_send(*info_args)
    exchange_wait_send(*cot_args)
    exchange_wait_send(*emb_args)


def result_kernel(*refs):
    count = len(refs) // 2
    for i in range(count):
        refs[count + i][...] = refs[i][...]


def dma(*shape):
    return pltpu.SemaphoreType.DMA(shape)


def vmem(shape, dtype=BF16):
    return pltpu.VMEM(shape, dtype)


def on_device(
    fields, var_ids, var_shift, var_scale, patch_weight, pos_table,
    layer_norm_gain, layer_norm_bias, order, grad_out,
):
    here = pl.BlockSpec(memory_space=pltpu.VMEM)
    scalars = pl.BlockSpec(memory_space=pltpu.SMEM)
    anywhere = pl.BlockSpec(memory_space=pl.ANY)
    shape = jax.ShapeDtypeStruct
    out_shape = (
        shape((1440, LANES), BF16),
        shape((20, E), F32),
        shape((45, 16, LANES), F32),
        shape((1, LANES), F32),
        shape((1, LANES), F32),
    )
    results = pl.pallas_call(
        encoder_kernel,
        out_shape=out_shape,
        in_specs=[scalars] * 3 + [anywhere] * 2 + [here] * 5,
        out_specs=(here,) * 5,
        scratch_shapes=[
            vmem((4, 10, 16, 1440)), vmem((640, E)),
            vmem((NB, 8, LANES), F32), vmem((NB, 8, LANES), F32), vmem((T, LANES), F32),
            vmem((8, T), F32), vmem((T, LANES), F32), vmem((8, T), F32),
            vmem((T, LANES)), vmem((T, LANES)), vmem((T, LANES)), vmem((T, LANES)),
            vmem((2, 4, 80, T)), vmem((E, E)), vmem((512, E)),
            vmem((640, 640)), vmem((640, 640)), vmem((640, T)), vmem((640, T)),
            vmem((PIECE, 640)), vmem((640, E)),
            vmem((4, T, 256)), vmem((T, 256)), vmem((T, 256)), vmem((T, 256)),
            vmem((T, LANES)), vmem((T, LANES)), vmem((LANES, LANES), F32), vmem((T, LANES), F32),
            vmem((T, LANES), F32), vmem((2, 8, PIECE), F32), vmem((2, 4, 8, PIECE), F32),
            vmem((2, 8, PIECE), F32), vmem((2, 8, PIECE), F32), vmem((2, PIECE, LANES), F32),
            vmem((T, LANES)), vmem((T, LANES)), vmem((T, LANES)), vmem((4, 2, T, LANES)),
            vmem((4, 320, 256)), vmem((4, 320, 256)), vmem((4, 320, 256), F32),
            vmem((4, 320, 256)), vmem((4, 3, 80, 256)),
            vmem((4, 128, 256)), vmem((4, 3, 32, 256)),
            vmem((48, LANES), F32), vmem((48, LANES), F32), vmem((48, LANES), F32),
            vmem((48, LANES), F32), vmem((48, LANES), F32), vmem((4, 4, 48, LANES), F32),
            dma(5), dma(NB), dma(NB), dma(NB), dma(NB),
            dma(4), dma(4), dma(4), dma(4), dma(4), dma(4), dma(4), dma(4),
            dma(2, 3), dma(2, 4), dma(2), dma(2), dma(NB), dma(NB), dma(4), dma(4),
            dma(2, 4, 2), dma(2, 4), dma(2, 4), dma(2, 4), dma(2, 4),
            dma(4), dma(4), dma(4, 3), dma(4, 3), dma(4, 3), dma(4, 3),
            dma(2), dma(2), dma(3), dma(3), dma(3), dma(3),
        ],
        compiler_params=pltpu.CompilerParams(
            has_side_effects=True, vmem_limit_bytes=58 * 1024 * 1024, collective_id=0
        ),
        name="encoder",
    )(
        var_ids, var_shift, var_scale, fields, patch_weight.reshape(640, E),
        pos_table.transpose(1, 0, 2), order.reshape(1, 1440), grad_out,
        layer_norm_gain.reshape(1, LANES), layer_norm_bias.reshape(1, LANES),
    )
    embed, grad_weight, grad_table, grad_gain, grad_bias = pl.pallas_call(
        result_kernel,
        out_shape=out_shape,
        in_specs=[here] * 5,
        out_specs=(here,) * 5,
        name="results",
    )(*results)
    return (
        embed, grad_weight, grad_table.transpose(1, 0, 2),
        grad_gain.reshape(LANES), grad_bias.reshape(LANES),
    )


def solution(mesh):
    in_specs = (
        P(None, "var", "band", None),
        P("var"),
        P(),
        P(),
        P("var", None, None),
        P(None, None, "var"),
        P("var"),
        P("var"),
        P("band"),
        P("band", "var"),
    )
    out_specs = (
        P("band", "var"),
        P(("var", "band"), None),
        P(None, None, "var"),
        P("var"),
        P("var"),
    )
    return jax.shard_map(
        on_device, mesh=mesh, in_specs=in_specs, out_specs=out_specs, check_vma=False
    )
```

```python
import functools

import jax
import jax.numpy as jnp
from jax import lax
from jax.experimental import pallas as pl
from jax.experimental.pallas import tpu as pltpu
from jax.sharding import PartitionSpec as P

EPS = 1e-05
T = 1536
LANES = 128
NB = 32
NV = 8
PER = 48
USED = 45
E = 1024
PIECE = 384
SENT = 368
F32 = jnp.float32
BF16 = jnp.bfloat16
HI = lax.Precision.HIGHEST


def iota(shape, dim):
    return lax.broadcasted_iota(jnp.int32, shape, dim)


def onehot(cond):
    return jnp.where(cond, 1.0, 0.0).astype(BF16)


def dot(a, b):
    return jnp.dot(a, b, preferred_element_type=F32)


def remote(src, dst, send, recv, v, b):
    return pltpu.make_async_remote_copy(
        src_ref=src,
        dst_ref=dst,
        send_sem=send,
        recv_sem=recv,
        device_id=(v, b),
        device_id_type=pl.DeviceIdType.MESH,
    )


class Place:
    def __init__(self):
        self.v = lax.axis_index("var")
        self.b = lax.axis_index("band")
        self.x = self.v // 2
        self.h = self.v % 2
        self.zl = self.b // 8
        self.y = (self.b // 2) % 4
        self.core = self.b % 2
        self.right = lax.rem(self.x + 1, 4) * 2 + self.h
        self.left = lax.rem(self.x + 3, 4) * 2 + self.h
        self.over = self.x * 2 + 1 - self.h

    def band_peer(self, k):
        return lax.rem(self.b + k, NB)

    def band_source(self, k):
        return lax.rem(self.b + NB - k, NB)


def greet(me, var_peers):
    barrier = pltpu.get_barrier_semaphore()

    @pl.loop(1, NB)
    def _(k):
        pl.semaphore_signal(
            barrier, inc=1, device_id=(me.v, me.band_peer(k)), device_id_type=pl.DeviceIdType.MESH
        )

    for peer in var_peers:
        pl.semaphore_signal(
            barrier, inc=1, device_id=(peer, me.b), device_id_type=pl.DeviceIdType.MESH
        )
    return lambda: pl.semaphore_wait(barrier, NB - 1 + len(var_peers))


def rows(i, n):
    return pl.ds(pl.multiple_of(i * n, n), n)


def exchange_start(me, src, dst, send, recv):
    @pl.loop(1, NB)
    def _(k):
        d = me.band_peer(k)
        remote(src(d), dst(me.b), send.at[d], recv.at[me.b], me.v, d).start()


def exchange_wait_recv(me, src, dst, send, recv):
    @pl.loop(1, NB)
    def _(k):
        s = me.band_source(k)
        remote(src(s), dst(s), send.at[s], recv.at[s], me.v, s).wait_recv()


def exchange_wait_send(me, src, dst, send, recv):
    @pl.loop(1, NB)
    def _(k):
        d = me.band_peer(k)
        remote(src(d), dst(d), send.at[d], recv.at[d], me.v, d).wait_send()


def mix_blocks(me, transposed):
    shape = (LANES, LANES)
    token = iota(shape, 1 if transposed else 0)
    cell = iota(shape, 0 if transposed else 1)
    second = cell >= 64
    j = jnp.where(second, cell - 64, cell)
    first = (me.b + 1) // 2 - 1

    def lat(p):
        u = jnp.clip(
            ((2 * me.b + p).astype(F32) + 0.5) / 4.0 - 0.5, 0.0, 15.0
        )
        w0 = jnp.maximum(1.0 - jnp.abs(u - first.astype(F32)), 0.0)
        w1 = jnp.maximum(1.0 - jnp.abs(u - (first + 1).astype(F32)), 0.0)
        return jnp.where(second, w1, w0)

    def lon(c):
        w = (c.astype(F32) + 0.5) / 4.0 - 0.5
        d = jnp.abs(w - j.astype(F32))
        d = jnp.minimum(d, 45.0 - d)
        return jnp.where(j < 45, jnp.maximum(1.0 - d, 0.0), 0.0)

    lat0, lat1 = lat(0), lat(1)
    low = lon(token)
    end0 = jnp.where(token < 52, lat0 * lon(token + 128), 0.0)
    end1 = jnp.where(
        jnp.logical_and(token >= 52, token < 104), lat1 * lon(token + 76), 0.0
    )
    return [(m).astype(BF16) for m in (lat0 * low, lat1 * low, end0 + end1)]


def nt(a, b):
    return lax.dot_general(a, b, (((1,), (1,)), ((), ())), preferred_element_type=F32)


def sample(s):
    return pl.ds(s * PIECE, PIECE)


def sent(s):
    return pl.ds(s * PIECE, SENT)


def half(s, f):
    return pl.ds(s * PIECE + 192 * f, 192 - 16 * f)


def encoder_kernel(
    ids, shift, scale, fields_at, weight_at, table, order, gout, gain_in, bias_in,
    embed, grad_weight, grad_table, grad_gain, grad_bias,
    fields, weight, info, got_info, slotcol, posrow, poscol, slotrow, gpad, cot_out, cot_in, cot,
    xn, sel, sel_end, perm, permb, xt, xb, xrow, wq, part, leg, from_left, from_right,
    zout, zin, window, pre,
    packed, sums_in, emb, emb_out, emb_in, dg,
    first, core_out, core_in, gw, y_out, y_in, zl_out, zl_in,
    outer, outer_in, inner, chip, chip_in, tables,
    load_s, info_s, info_r, cot_s, cot_r, leg_s, leg_r, dir_s, comb_s, left_r, right_r, z_s, z_r,
    sum_s, sum_r, emb_s, emb_r, dz_s, dz_r, dx_s, dr_r, dl_r, df_s, df_r,
    core_s, core_r, y_s, y_r, zl_s, zl_r, t_s, t_r, tz_s, tz_r, ty_s, ty_r,
):
    me = Place()
    wait_barrier = greet(me, [lax.rem(me.v + k, NV) for k in range(1, NV)])
    gain = gain_in[...]
    bias = bias_in[...]
    sends = []

    def send(copy):
        copy.start()
        sends.append(copy)

    loads = [pltpu.make_async_copy(weight_at, weight, load_s.at[4])]
    for s in range(4):
        loads.append(pltpu.make_async_copy(fields_at.at[s], fields.at[s], load_s.at[s]))
    for copy in loads:
        copy.start()

    info_args = (me, lambda d: info.at[d], lambda s: got_info.at[s], info_s, info_r)

    def ask():
        o = order[...].reshape(1, 1440).astype(F32)
        pieces = []
        for s in range(4):
            at = 360 * s
            pieces += [o[:, at : at + 128], o[:, at + 180 : at + 308]]
            pieces.append(
                jnp.concatenate(
                    [o[:, at + 128 : at + 180], o[:, at + 308 : at + 360],
                     jnp.full((1, 24), 99.0 * 1440.0, F32)], 1
                )
            )
        o = jnp.concatenate(pieces, 1)
        target = jnp.floor((o + 0.5) * (1.0 / 1440.0))
        slot = o - target * 1440.0
        high = jnp.floor(slot * (1.0 / 32.0))
        low = slot - high * 32.0
        to_shard = jnp.where(iota((NB, T), 0).astype(F32) == target, 1.0, 0.0)
        tiles = [to_shard[:, i * 128 : i * 128 + 128] for i in range(12)]
        above = onehot(iota((LANES, LANES), 0) < iota((LANES, LANES), 1))
        before = dot(jnp.concatenate(tiles, 0).astype(BF16), above)
        carry = jnp.zeros((NB, 1), F32)
        ranks = []
        for i in range(12):
            ranks.append(
                jnp.sum(tiles[i] * (before[i * NB : i * NB + NB] + carry), 0, keepdims=True)
            )
            carry = carry + jnp.sum(tiles[i], 1, keepdims=True)
        rank = jnp.concatenate(ranks, 1)
        posrow[...] = jnp.broadcast_to(target * PER + rank, (8, T))
        at = iota((LANES, T), 0).astype(F32) == rank
        shards = to_shard.astype(BF16)
        slots = nt(shards, jnp.where(at, high, 0.0).astype(BF16)) * 32.0 + nt(
            shards, jnp.where(at, low, 0.0).astype(BF16)
        )
        slots = jnp.where(iota((NB, LANES), 1) < USED, slots, -1.0)
        for d in range(NB):
            info[d] = jnp.broadcast_to(slots[d : d + 1], (8, LANES))
        wait_barrier()
        exchange_start(*info_args)
        got_info[pl.ds(me.b, 1)] = info[pl.ds(me.b, 1)]

    xn[:, :, :, 1408:1536] = jnp.zeros((2, 4, 80, 128), BF16)
    for s in range(4):
        pad = slice(s * PIECE + SENT, (s + 1) * PIECE)
        zero = jnp.zeros((PIECE - SENT, 256), BF16)
        from_left[pad, :] = zero
        from_right[pad, :] = zero
        zin[pad, :] = zero[:, 0:128]
        for c in range(4):
            for hh in range(2):
                dg[c, hh, pad, :] = zero[:, 0:128]

    @pl.loop(0, 8)
    def _(i):
        n = iota((LANES, E), 1)
        k = iota((LANES, E), 0) + i * LANES
        sel[rows(i, LANES), :] = onehot(k == (n & 127) * 8 + (n >> 7))

    @pl.loop(0, 4)
    def _(i):
        n = iota((LANES, E), 1)
        k = iota((LANES, E), 0) + i * LANES
        sel_end[rows(i, LANES), :] = onehot(k == ((n & 127) - 52) * 8 + (n >> 7))

    n = iota((80, 640), 1)
    g = iota((80, 640), 0)
    for dx in range(8):
        perm[dx * 80 : dx * 80 + 80, :] = onehot(n == g * 8 + dx)
    loads[0].wait()
    for i in range(4):
        lanes = slice(i * 256, i * 256 + 256)
        wq[:, lanes] = dot(perm[...], weight[:, lanes]).astype(BF16)
    eye = onehot(iota((PIECE, PIECE), 0) == iota((PIECE, PIECE), 1))

    def patches(ch):
        for s in (2 * ch, 2 * ch + 1):
            loads[1 + s].wait()

            @pl.loop(0, 5)
            def _(pair):
                halves = []
                for j in range(2):
                    k = 2 * pair + j
                    at = ids[k]
                    halves.append((fields[s, k].astype(F32) - shift[at]) * scale[at])
                for p in range(2):
                    both = jnp.concatenate([q[8 * p : 8 * p + 8] for q in halves], 0)
                    xn[p, s, rows(pair, 16), 0:1440] = both.astype(BF16)

        x = [xn[p, 2 * ch : 2 * ch + 2].reshape(160, T) for p in range(2)]
        both = jnp.concatenate(x, 0)
        for i in range(4):
            out = slice(i * 256, i * 256 + 256)
            low = dot(both[:, 0:1024], sel[:, out]).astype(BF16)
            end = (
                dot(x[0][:, 1024:1536], sel[0:512, out])
                + dot(x[1][:, 1024:1536], sel_end[:, out])
            ).astype(BF16)
            for q in range(2):
                at = slice((2 * i + q) * 80, (2 * i + q) * 80 + 80)
                lanes = slice(q * 128, q * 128 + 128)
                for s in range(2):
                    base = (2 * ch + s) * PIECE
                    for p in range(2):
                        first = (2 * p + s) * 80
                        xt[at, base + p * 128 : base + p * 128 + 128] = low[
                            first : first + 80, lanes
                        ]
                    xt[at, base + 256 : base + 384] = end[s * 80 : s * 80 + 80, lanes]

    def partials(s):
        xrow[...] = nt(eye, xt[:, sample(s)]).astype(BF16)
        for j, ahead in ((0, 2), (1, 1), (2, 3), (3, 0)):
            at = lax.rem(me.x + ahead, 4)
            lanes = pl.ds(pl.multiple_of(at * 256, 256), 256)
            part[j, sample(s), :] = dot(xrow[...], wq[:, lanes]).astype(BF16)

    def start_x(s):
        for f in range(2):
            ahead, back = (me.right, me.left) if f == 0 else (me.left, me.right)
            at = half(s, f)
            send(remote(part.at[0, at], leg.at[at], leg_s.at[s, f], leg_r.at[s, f], ahead, me.b))
            src, into, sem = (part.at[2], from_right, right_r) if f == 0 else (
                part.at[1], from_left, left_r)
            send(remote(src.at[at], into.at[at], dir_s.at[s, f], sem.at[s, f], back, me.b))

    def pass_on(s):
        for f in range(2):
            ahead, back = (me.right, me.left) if f == 0 else (me.left, me.right)
            at = half(s, f)
            remote(part.at[0, at], leg.at[at], leg_s.at[s, f], leg_r.at[s, f],
                   back, me.b).wait_recv()
            j = 1 + f
            part[j, at, :] = (part[j, at, :].astype(F32) + leg[at, :].astype(F32)).astype(BF16)
            into, sem = (from_left, left_r) if f == 0 else (from_right, right_r)
            send(remote(part.at[j, at], into.at[at], comb_s.at[s, f], sem.at[s, f], ahead, me.b))

    def finish_x(s):
        for f in range(2):
            at = half(s, f)
            src = part.at[0, at]
            remote(src, from_left.at[at], dir_s.at[s, f], left_r.at[s, f],
                   me.left, me.b).wait_recv()
            remote(src, from_right.at[at], dir_s.at[s, f], right_r.at[s, f],
                   me.right, me.b).wait_recv()
        sl = sample(s)
        total = (
            part[3, sl, :].astype(F32) + from_left[sl, :].astype(F32)
        ) + from_right[sl, :].astype(F32)
        mine = jnp.where(me.h == 0, total[:, 0:128], total[:, 128:256])
        other = jnp.where(me.h == 0, total[:, 128:256], total[:, 0:128])
        zout[sl, :] = other.astype(BF16)
        send(remote(zout.at[sent(s)], zin.at[sent(s)], z_s.at[s], z_r.at[s], me.over, me.b))
        pre[sl, :] = mine

    def finish_z(s):
        remote(zout.at[sent(s)], zin.at[sent(s)], z_s.at[s], z_r.at[s], me.over, me.b).wait_recv()
        sl = sample(s)
        pre[sl, :] = pre[sl, :] + zin[sl, :].astype(F32) + jnp.concatenate(position, 0)

    cot_args = (
        me,
        lambda d: cot_out.at[rows(d, PER)],
        lambda s: cot_in.at[rows(s, PER)],
        cot_s,
        cot_r,
    )
    wide = iota((384, T), 1).astype(F32)

    def answer():
        gpad[1440:T, :] = jnp.zeros((T - 1440, LANES), BF16)
        gpad[0:1440, :] = gout[...]
        exchange_wait_recv(*info_args)
        asked = jnp.concatenate([got_info[s][0:1] for s in range(NB)], 0)
        asked = jnp.concatenate([asked, jnp.zeros((LANES - NB, LANES), F32)], 0).T
        for i in range(4):
            at = jnp.concatenate([asked[0:PER, s : s + 1] for s in range(8 * i, 8 * i + 8)], 0)
            slotcol[i * 384 : i * 384 + 384, :] = jnp.broadcast_to(at, (384, LANES))
            cot_out[i * 384 : i * 384 + 384, :] = dot(onehot(at == wide), gpad[...]).astype(BF16)
        exchange_start(*cot_args)
        cot_in[rows(me.b, PER), :] = cot_out[rows(me.b, PER), :]

    def place_cot():
        exchange_wait_recv(*cot_args)
        for i in range(4):
            sl = slice(i * 384, i * 384 + 384)
            cot[sl, :] = dot(onehot(poscol[sl, 0:1] == wide), cot_in[...]).astype(BF16)

    def local_sums(s):
        sl = sample(s)
        lane = iota((PIECE, LANES), 1)
        lane = jnp.where(iota((PIECE, LANES), 0) < 256, lane, lane - 4)
        a = pre[sl, :]
        g = cot[sl, :].astype(F32) * gain
        block = jnp.zeros((PIECE, LANES), F32)
        for k, q in enumerate((a, a * a, g, g * a)):
            block = jnp.where(lane == k, jnp.sum(q, 1, keepdims=True), block)
        flat = block.T[0:8]
        packed[s, :, 0:128] = flat[:, 0:128] + flat[:, 256:384]
        packed[s, :, 128:256] = flat[:, 128:256]
        sums_in[s, pl.ds(me.v, 1)] = packed[s][None]
        for k in range(1, NV):
            send(remote(packed.at[s], sums_in.at[s, me.v], sum_s.at[s, k - 1],
                        sum_r.at[s, me.v], lax.rem(me.v + k, NV), me.b))

    def all_sums(s):
        for k in range(1, NV):
            src = lax.rem(me.v + NV - k, NV)
            remote(packed.at[s], sums_in.at[s, src], sum_s.at[s, k - 1], sum_r.at[s, src],
                   src, me.b).wait_recv()
        total = sums_in[s, 0]
        for k in range(1, NV):
            total = total + sums_in[s, k]
        return jnp.concatenate([total, jnp.zeros((120, 256), F32)], 0).T

    own = dg.at[0, me.h]
    over = dg.at[0, 1 - me.h]
    totals = [jnp.zeros((1, LANES), F32), jnp.zeros((1, LANES), F32)]

    def send_x(block, hh, s):
        at = sent(s)
        send(remote(block.at[at], dg.at[1, hh, at], dx_s.at[hh, s, 0], dr_r.at[hh, s],
                    me.right, me.b))
        send(remote(block.at[at], dg.at[2, hh, at], dx_s.at[hh, s, 1], dl_r.at[hh, s],
                    me.left, me.b))

    def norm(s):
        col = all_sums(s)
        sl = sample(s)
        s1, s2, sg, sq = [
            jnp.concatenate([col[:, k : k + 1], col[0:128, 4 + k : 5 + k]], 0) for k in range(4)
        ]
        mean = s1 / E
        inv = lax.rsqrt(s2 / E - mean * mean + EPS)
        xhat = (pre[sl, :] - mean) * inv
        up = cot[sl, :].astype(F32)
        along = inv * (sq - mean * sg) / E
        d = inv * (up * gain - sg / E - xhat * along)
        own[sl, :] = d.astype(BF16)
        send(remote(own.at[sent(s)], own.at[sent(s)], dz_s.at[s], dz_r.at[s], me.over, me.b))
        send_x(own, me.h, s)
        emb[sl, :] = (xhat * gain + bias).astype(BF16)
        totals[0] = totals[0] + jnp.sum(up * xhat, 0, keepdims=True)
        totals[1] = totals[1] + jnp.sum(up, 0, keepdims=True)

    def over_arrives(s):
        remote(own.at[sent(s)], over.at[sent(s)], dz_s.at[s], dz_r.at[s], me.over, me.b).wait_recv()
        send_x(over, 1 - me.h, s)

    def pass_d(hh, s):
        at = sent(s)
        src = dg.at[0, hh, at]
        remote(src, dg.at[1, hh, at], dx_s.at[hh, s, 0], dr_r.at[hh, s], me.left, me.b).wait_recv()
        at = half(s, 0)
        send(remote(dg.at[1, hh, at], dg.at[3, hh, at], df_s.at[hh, s, 0], df_r.at[hh, s, 0],
                    me.right, me.b))
        at = sent(s)
        remote(src, dg.at[2, hh, at], dx_s.at[hh, s, 1], dl_r.at[hh, s], me.right, me.b).wait_recv()
        at = half(s, 1)
        send(remote(dg.at[2, hh, at], dg.at[3, hh, at], df_s.at[hh, s, 1], df_r.at[hh, s, 1],
                    me.left, me.b))

    def await_d(samples):
        for s in samples:
            for hh in range(2):
                for f in range(2):
                    at = half(s, f)
                    remote(dg.at[0, hh, at], dg.at[3, hh, at], df_s.at[hh, s, f],
                           df_r.at[hh, s, f], me.left, me.b).wait_recv()

    tall = iota((384, T), 0).astype(F32)
    emb_args = (
        me,
        lambda d: emb_out.at[rows(d, PER)],
        lambda s: emb_in.at[rows(s, PER)],
        emb_s,
        emb_r,
    )

    def pick_emb():
        for i in range(4):
            hot = onehot(posrow[0:1, :] == tall + i * 384.0)
            emb_out[i * 384 : i * 384 + 384, :] = dot(hot, emb[...]).astype(BF16)

    def start_emb():
        exchange_start(*emb_args)
        emb_in[rows(me.b, PER), :] = emb_out[rows(me.b, PER), :]

    def place_emb():
        exchange_wait_recv(*emb_args)
        for i in range(3):
            hot = onehot(slotrow[0:1, :] == iota((480, T), 0).astype(F32) + i * 480.0)
            embed[i * 480 : i * 480 + 480, :] = dot(hot, emb_in[...]).astype(BF16)

    even = me.core == 0
    across = jnp.where(even, lax.rem(me.b + NB - 1, NB), lax.rem(me.b + 1, NB))
    mate = jnp.where(even, me.b + 1, me.b - 1)
    outer_copy = remote(outer, outer_in, t_s.at[0], t_r.at[0], me.v, across)
    chip_copy = remote(chip, chip_in, t_s.at[1], t_r.at[1], me.v, mate)

    def table_rows():
        mixes = mix_blocks(me, True)
        term = jnp.zeros((LANES, LANES), F32)
        for i in range(12):
            term = term + dot(mixes[i % 3], own[i * LANES : (i + 1) * LANES, :])
        outer[...] = jnp.where(even, term[0:48], term[64:112])
        inner[...] = jnp.where(even, term[64:112], term[0:48])
        send(outer_copy)

    def table_chip():
        outer_copy.wait_recv()
        at = iota((48, LANES), 0)
        both = inner[...] + outer_in[...]
        chip[...] = jnp.where(at == 45, totals[0], jnp.where(at == 46, totals[1], both))
        send(chip_copy)

    def table_z():
        chip_copy.wait_recv()
        tables[pl.ds(me.y, 1), pl.ds(me.zl, 1)] = (chip[...] + chip_in[...])[None, None]
        for k in range(1, 4):
            to = lax.rem(me.zl + k, 4)
            here = tables.at[me.y, me.zl]
            send(remote(here, here, tz_s.at[k - 1], tz_r.at[k - 1],
                        me.v, to * 8 + me.y * 2 + me.core))

    def table_y():
        for k in range(1, 4):
            src = lax.rem(me.zl + 4 - k, 4)
            there = tables.at[me.y, src]
            remote(there, there, tz_s.at[k - 1], tz_r.at[k - 1],
                   me.v, src * 8 + me.y * 2 + me.core).wait_recv()
        for k in range(1, 4):
            to = lax.rem(me.y + k, 4)
            here = tables.at[me.y]
            send(remote(here, here, ty_s.at[k - 1], ty_r.at[k - 1],
                        me.v, me.zl * 8 + to * 2 + me.core))

    def table_end():
        for k in range(1, 4):
            src = lax.rem(me.y + 4 - k, 4)
            there = tables.at[src]
            remote(there, there, ty_s.at[k - 1], ty_r.at[k - 1],
                   me.v, me.zl * 8 + src * 2 + me.core).wait_recv()
        gain_total = jnp.zeros((1, LANES), F32)
        bias_total = jnp.zeros((1, LANES), F32)
        for i in range(16):
            block = tables[i % 4, i // 4]
            grad_table[:, i, :] = block[0:45]
            gain_total = gain_total + block[45:46]
            bias_total = bias_total + block[46:47]
        grad_gain[...] = gain_total
        grad_bias[...] = bias_total

    mate_core = 1 - me.core

    late = slice(3 * PIECE, T)

    def early(c):
        right = jnp.concatenate([dg[c, 0, 0 : 3 * PIECE], dg[c, 1, 0 : 3 * PIECE]], 1)
        first[c] = dot(xb[:, 0 : 3 * PIECE], right)

    def multiply(c):
        right = jnp.concatenate([dg[c, 0, late], dg[c, 1, late]], 1)
        theirs = pl.ds(pl.multiple_of(mate_core * 320, 320), 320)
        core_out[c] = (first[c, theirs, :] + dot(xb[theirs, late], right)).astype(BF16)
        send(remote(core_out.at[c], core_in.at[c], core_s.at[c], core_r.at[c], me.v, mate))
        mine = pl.ds(pl.multiple_of(me.core * 320, 320), 320)
        gw[c] = first[c, mine, :] + dot(xb[mine, late], right)

    def over_y(c):
        remote(core_out.at[c], core_in.at[c], core_s.at[c], core_r.at[c], me.v, mate).wait_recv()
        y_out[c] = (gw[c] + core_in[c].astype(F32)).astype(BF16)
        for k in range(1, 4):
            to = lax.rem(me.y + k, 4)
            src = y_out.at[c, rows(to, 80)]
            send(remote(src, y_in.at[c, k - 1], y_s.at[c, k - 1], y_r.at[c, k - 1],
                        me.v, me.zl * 8 + to * 2 + me.core))

    spread_r = iota((128, 80), 0)
    spread_c = iota((128, 80), 1)
    inside = spread_r & 31
    spread = onehot(
        jnp.logical_and(inside < 20, spread_c == (spread_r >> 5) * 20 + inside)
    )

    def over_z(c):
        total = y_out[c, rows(me.y, 80), :].astype(F32)
        for k in range(1, 4):
            src = lax.rem(me.y + 4 - k, 4)
            remote(y_out.at[c, rows(src, 80)], y_in.at[c, k - 1], y_s.at[c, k - 1],
                   y_r.at[c, k - 1], me.v, me.zl * 8 + src * 2 + me.core).wait_recv()
            total = total + y_in[c, k - 1].astype(F32)
        zl_out[c] = dot(spread, total.astype(BF16)).astype(BF16)
        for k in range(1, 4):
            to = lax.rem(me.zl + k, 4)
            send(remote(zl_out.at[c, rows(to, 32)], zl_in.at[c, k - 1], zl_s.at[c, k - 1],
                        zl_r.at[c, k - 1], me.v, to * 8 + me.y * 2 + me.core))

    def finish(c):
        total = zl_out[c, rows(me.zl, 32), :].astype(F32)
        for k in range(1, 4):
            src = lax.rem(me.zl + 4 - k, 4)
            remote(zl_out.at[c, rows(src, 32)], zl_in.at[c, k - 1], zl_s.at[c, k - 1],
                   zl_r.at[c, k - 1], me.v, src * 8 + me.y * 2 + me.core).wait_recv()
            total = total + zl_in[c, k - 1].astype(F32)
        x = lax.rem(me.x + (0, 3, 1, 2)[c], 4)
        grad_weight[:, pl.ds(pl.multiple_of(x * 256, 256), 256)] = total[0:20]

    ask()
    patches(0)
    partials(0)
    start_x(0)
    partials(1)
    start_x(1)
    answer()
    pass_on(0)
    patches(1)
    partials(2)
    start_x(2)
    pass_on(1)
    partials(3)
    start_x(3)

    low_row = (me.b + 1) // 2 - 1
    window[...] = jnp.zeros((LANES, LANES), F32)
    level = iota((45, 16, LANES), 1)
    all_rows = table[...]
    window[0:45, :] = jnp.sum(jnp.where(level == low_row, all_rows, 0.0), 1)
    window[64:109, :] = jnp.sum(jnp.where(level == low_row + 1, all_rows, 0.0), 1)
    position = [
        jnp.dot(m.astype(F32), window[...], precision=HI, preferred_element_type=F32)
        for m in mix_blocks(me, False)
    ]
    poscol[...] = jnp.concatenate([posrow[...], jnp.zeros((120, T), F32)], 0).T

    finish_x(0)
    pass_on(2)

    r = iota((640, 1), 0)

    def steps(a, size, count):
        at = jnp.zeros_like(a)
        for i in range(1, count):
            at = at + jnp.where(a >= i * size, 1, 0)
        return at

    core = steps(r, 320, 2)
    r = r - 320 * core
    y = steps(r, 80, 4)
    r = r - 80 * y
    zl = steps(r, 20, 4)
    n = 20 * (zl * 8 + y * 2 + core) + r - 20 * zl
    permb[...] = onehot(iota((640, 640), 1) == (n & 7) * 80 + (n >> 3))

    def arrange(s):
        xb[:, sample(s)] = dot(permb[...], xt[:, sample(s)]).astype(BF16)

    arrange(0)
    finish_x(1)
    pass_on(3)
    arrange(1)
    place_cot()
    finish_x(2)
    finish_z(0)
    local_sums(0)
    finish_x(3)
    finish_z(1)
    local_sums(1)
    finish_z(2)
    local_sums(2)
    finish_z(3)
    local_sums(3)
    norm(0)
    norm(1)
    arrange(2)
    arrange(3)
    norm(2)
    norm(3)
    pass_d(me.h, 0)
    pass_d(me.h, 1)
    over_arrives(0)
    over_arrives(1)
    pass_d(1 - me.h, 0)
    pass_d(1 - me.h, 1)
    for i in range(12):
        sl = slice(i * LANES, (i + 1) * LANES)
        slotrow[:, sl] = slotcol[sl, :].T[0:8]
    pick_emb()
    over_arrives(2)
    pass_d(me.h, 2)
    early(0)
    table_rows()
    over_arrives(3)
    pass_d(me.h, 3)
    start_emb()
    multiply(0)
    pass_d(1 - me.h, 2)
    early(1)
    over_y(0)
    table_chip()
    early(2)
    pass_d(1 - me.h, 3)
    multiply(1)
    multiply(2)
    await_d(range(3))
    early(3)
    over_z(0)
    over_y(1)
    over_y(2)
    table_z()
    await_d(range(3, 4))
    multiply(3)
    over_z(1)
    over_z(2)
    over_y(3)
    table_y()
    finish(0)
    place_emb()
    over_z(3)
    finish(1)
    finish(2)
    table_end()
    finish(3)
    for copy in sends:
        copy.wait_send()
    exchange_wait_send(*info_args)
    exchange_wait_send(*cot_args)
    exchange_wait_send(*emb_args)


def result_kernel(*refs):
    count = len(refs) // 2
    for i in range(count):
        refs[count + i][...] = refs[i][...]


def dma(*shape):
    return pltpu.SemaphoreType.DMA(shape)


def vmem(shape, dtype=BF16):
    return pltpu.VMEM(shape, dtype)


def on_device(
    fields, var_ids, var_shift, var_scale, patch_weight, pos_table,
    layer_norm_gain, layer_norm_bias, order, grad_out,
):
    here = pl.BlockSpec(memory_space=pltpu.VMEM)
    scalars = pl.BlockSpec(memory_space=pltpu.SMEM)
    anywhere = pl.BlockSpec(memory_space=pl.ANY)
    shape = jax.ShapeDtypeStruct
    out_shape = (
        shape((1440, LANES), BF16),
        shape((20, E), F32),
        shape((45, 16, LANES), F32),
        shape((1, LANES), F32),
        shape((1, LANES), F32),
    )
    results = pl.pallas_call(
        encoder_kernel,
        out_shape=out_shape,
        in_specs=[scalars] * 3 + [anywhere] * 2 + [here] * 5,
        out_specs=(here,) * 5,
        scratch_shapes=[
            vmem((4, 10, 16, 1440)), vmem((640, E)),
            vmem((NB, 8, LANES), F32), vmem((NB, 8, LANES), F32), vmem((T, LANES), F32),
            vmem((8, T), F32), vmem((T, LANES), F32), vmem((8, T), F32),
            vmem((T, LANES)), vmem((T, LANES)), vmem((T, LANES)), vmem((T, LANES)),
            vmem((2, 4, 80, T)), vmem((E, E)), vmem((512, E)),
            vmem((640, 640)), vmem((640, 640)), vmem((640, T)), vmem((640, T)),
            vmem((PIECE, 640)), vmem((640, E)),
            vmem((4, T, 256)), vmem((T, 256)), vmem((T, 256)), vmem((T, 256)),
            vmem((T, LANES)), vmem((T, LANES)), vmem((LANES, LANES), F32), vmem((T, LANES), F32),
            vmem((4, 8, 256), F32), vmem((4, NV, 8, 256), F32),
            vmem((T, LANES)), vmem((T, LANES)), vmem((T, LANES)), vmem((4, 2, T, LANES)),
            vmem((4, 640, 256), F32),
            vmem((4, 320, 256)), vmem((4, 320, 256)), vmem((4, 320, 256), F32),
            vmem((4, 320, 256)), vmem((4, 3, 80, 256)),
            vmem((4, 128, 256)), vmem((4, 3, 32, 256)),
            vmem((48, LANES), F32), vmem((48, LANES), F32), vmem((48, LANES), F32),
            vmem((48, LANES), F32), vmem((48, LANES), F32), vmem((4, 4, 48, LANES), F32),
            dma(5), dma(NB), dma(NB), dma(NB), dma(NB),
            dma(4, 2), dma(4, 2), dma(4, 2), dma(4, 2), dma(4, 2), dma(4, 2), dma(4), dma(4),
            dma(4, 7), dma(4, NV), dma(NB), dma(NB), dma(4), dma(4),
            dma(2, 4, 2), dma(2, 4), dma(2, 4), dma(2, 4, 2), dma(2, 4, 2),
            dma(4), dma(4), dma(4, 3), dma(4, 3), dma(4, 3), dma(4, 3),
            dma(2), dma(2), dma(3), dma(3), dma(3), dma(3),
        ],
        compiler_params=pltpu.CompilerParams(
            has_side_effects=True, vmem_limit_bytes=58 * 1024 * 1024, collective_id=0
        ),
        name="encoder",
    )(
        var_ids, var_shift, var_scale, fields, patch_weight.reshape(640, E),
        pos_table.transpose(1, 0, 2), order, grad_out,
        layer_norm_gain.reshape(1, LANES), layer_norm_bias.reshape(1, LANES),
    )
    embed, grad_weight, grad_table, grad_gain, grad_bias = pl.pallas_call(
        result_kernel,
        out_shape=out_shape,
        in_specs=[here] * 5,
        out_specs=(here,) * 5,
        name="results",
    )(*results)
    return (
        embed, grad_weight, grad_table.transpose(1, 0, 2),
        grad_gain.reshape(LANES), grad_bias.reshape(LANES),
    )


def solution(mesh):
    in_specs = (
        P(None, "var", "band", None),
        P("var"),
        P(),
        P(),
        P("var", None, None),
        P(None, None, "var"),
        P("var"),
        P("var"),
        P("band"),
        P("band", "var"),
    )
    out_specs = (
        P("band", "var"),
        P(("var", "band"), None),
        P(None, None, "var"),
        P("var"),
        P("var"),
    )
    return jax.shard_map(
        on_device, mesh=mesh, in_specs=in_specs, out_specs=out_specs, check_vma=False
    )
```

```python
import functools

import jax
import jax.numpy as jnp
from jax import lax
from jax.experimental import pallas as pl
from jax.experimental.pallas import tpu as pltpu
from jax.sharding import PartitionSpec as P

EPS = 1e-05
T = 1536
LANES = 128
NB = 32
NV = 8
PER = 48
USED = 45
E = 1024
PIECE = 384
SENT = 368
F32 = jnp.float32
BF16 = jnp.bfloat16
HI = lax.Precision.HIGHEST


def iota(shape, dim):
    return lax.broadcasted_iota(jnp.int32, shape, dim)


def onehot(cond):
    return jnp.where(cond, 1.0, 0.0).astype(BF16)


def dot(a, b):
    return jnp.dot(a, b, preferred_element_type=F32)


def remote(src, dst, send, recv, v, b):
    return pltpu.make_async_remote_copy(
        src_ref=src,
        dst_ref=dst,
        send_sem=send,
        recv_sem=recv,
        device_id=(v, b),
        device_id_type=pl.DeviceIdType.MESH,
    )


class Place:
    def __init__(self):
        self.v = lax.axis_index("var")
        self.b = lax.axis_index("band")
        self.x = self.v // 2
        self.h = self.v % 2
        self.zl = self.b // 8
        self.y = (self.b // 2) % 4
        self.core = self.b % 2
        self.right = lax.rem(self.x + 1, 4) * 2 + self.h
        self.left = lax.rem(self.x + 3, 4) * 2 + self.h
        self.over = self.x * 2 + 1 - self.h

    def band_peer(self, k):
        return lax.rem(self.b + k, NB)

    def band_source(self, k):
        return lax.rem(self.b + NB - k, NB)


def greet(me, var_peers):
    barrier = pltpu.get_barrier_semaphore()

    @pl.loop(1, NB)
    def _(k):
        pl.semaphore_signal(
            barrier, inc=1, device_id=(me.v, me.band_peer(k)), device_id_type=pl.DeviceIdType.MESH
        )

    for peer in var_peers:
        pl.semaphore_signal(
            barrier, inc=1, device_id=(peer, me.b), device_id_type=pl.DeviceIdType.MESH
        )
    return lambda: pl.semaphore_wait(barrier, NB - 1 + len(var_peers))


def rows(i, n):
    return pl.ds(pl.multiple_of(i * n, n), n)


def exchange_start(me, src, dst, send, recv):
    @pl.loop(1, NB)
    def _(k):
        d = me.band_peer(k)
        remote(src(d), dst(me.b), send.at[d], recv.at[me.b], me.v, d).start()


def exchange_wait_recv(me, src, dst, send, recv):
    @pl.loop(1, NB)
    def _(k):
        s = me.band_source(k)
        remote(src(s), dst(s), send.at[s], recv.at[s], me.v, s).wait_recv()


def exchange_wait_send(me, src, dst, send, recv):
    @pl.loop(1, NB)
    def _(k):
        d = me.band_peer(k)
        remote(src(d), dst(d), send.at[d], recv.at[d], me.v, d).wait_send()


def mix_blocks(me, transposed):
    shape = (LANES, LANES)
    token = iota(shape, 1 if transposed else 0)
    cell = iota(shape, 0 if transposed else 1)
    second = cell >= 64
    j = jnp.where(second, cell - 64, cell)
    first = (me.b + 1) // 2 - 1

    def lat(p):
        u = jnp.clip(
            ((2 * me.b + p).astype(F32) + 0.5) / 4.0 - 0.5, 0.0, 15.0
        )
        w0 = jnp.maximum(1.0 - jnp.abs(u - first.astype(F32)), 0.0)
        w1 = jnp.maximum(1.0 - jnp.abs(u - (first + 1).astype(F32)), 0.0)
        return jnp.where(second, w1, w0)

    def lon(c):
        w = (c.astype(F32) + 0.5) / 4.0 - 0.5
        d = jnp.abs(w - j.astype(F32))
        d = jnp.minimum(d, 45.0 - d)
        return jnp.where(j < 45, jnp.maximum(1.0 - d, 0.0), 0.0)

    lat0, lat1 = lat(0), lat(1)
    low = lon(token)
    end0 = jnp.where(token < 52, lat0 * lon(token + 128), 0.0)
    end1 = jnp.where(
        jnp.logical_and(token >= 52, token < 104), lat1 * lon(token + 76), 0.0
    )
    return [(m).astype(BF16) for m in (lat0 * low, lat1 * low, end0 + end1)]


def nt(a, b):
    return lax.dot_general(a, b, (((1,), (1,)), ((), ())), preferred_element_type=F32)


def sample(s):
    return pl.ds(s * PIECE, PIECE)


def sent(s):
    return pl.ds(s * PIECE, SENT)


def half(s, f):
    return pl.ds(s * PIECE + 192 * f, 192 - 16 * f)


def encoder_kernel(
    ids, shift, scale, fields_at, weight_at, table_at, gout_at, order, gain_in, bias_in,
    embed, grad_weight, grad_table, grad_gain, grad_bias,
    fields, weight, table, info, got_info, slotcol, posrow, poscol, slotrow, gpad, cot_out, cot_in, cot,
    xn, sel, sel_end, perm, permb, xt, xb, xrow, wq, part, leg, from_left, from_right,
    zout, zin, window, pre,
    packed, sums_in, emb, emb_out, emb_in, dg,
    first, core_out, core_in, gw, y_out, y_in, zl_out, zl_in,
    outer, outer_in, inner, chip, chip_in, tables,
    load_s, info_s, info_r, cot_s, cot_r, leg_s, leg_r, dir_s, comb_s, left_r, right_r, z_s, z_r,
    sum_s, sum_r, emb_s, emb_r, dz_s, dz_r, dx_s, dr_r, dl_r, df_s, df_r,
    core_s, core_r, y_s, y_r, zl_s, zl_r, t_s, t_r, tz_s, tz_r, ty_s, ty_r,
):
    me = Place()
    wait_barrier = greet(me, [lax.rem(me.v + k, NV) for k in range(1, NV)])
    gain = gain_in[...]
    bias = bias_in[...]
    sends = []

    def send(copy):
        copy.start()
        sends.append(copy)

    loads = [pltpu.make_async_copy(weight_at, weight, load_s.at[4])]
    for s in range(4):
        loads.append(pltpu.make_async_copy(fields_at.at[s], fields.at[s], load_s.at[s]))
    for copy in loads:
        copy.start()
    gout_load = pltpu.make_async_copy(gout_at, gpad.at[pl.ds(0, 1440)], load_s.at[5])
    table_load = pltpu.make_async_copy(table_at, table, load_s.at[6])
    gout_load.start()
    table_load.start()

    info_args = (me, lambda d: info.at[d], lambda s: got_info.at[s], info_s, info_r)

    def ask():
        o = order[...].reshape(1, 1440).astype(F32)
        pieces = []
        for s in range(4):
            at = 360 * s
            pieces += [o[:, at : at + 128], o[:, at + 180 : at + 308]]
            pieces.append(
                jnp.concatenate(
                    [o[:, at + 128 : at + 180], o[:, at + 308 : at + 360],
                     jnp.full((1, 24), 99.0 * 1440.0, F32)], 1
                )
            )
        o = jnp.concatenate(pieces, 1)
        target = jnp.floor((o + 0.5) * (1.0 / 1440.0))
        slot = o - target * 1440.0
        high = jnp.floor(slot * (1.0 / 32.0))
        low = slot - high * 32.0
        to_shard = jnp.where(iota((NB, T), 0).astype(F32) == target, 1.0, 0.0)
        tiles = [to_shard[:, i * 128 : i * 128 + 128] for i in range(12)]
        above = onehot(iota((LANES, LANES), 0) < iota((LANES, LANES), 1))
        before = dot(jnp.concatenate(tiles, 0).astype(BF16), above)
        carry = jnp.zeros((NB, 1), F32)
        ranks = []
        for i in range(12):
            ranks.append(
                jnp.sum(tiles[i] * (before[i * NB : i * NB + NB] + carry), 0, keepdims=True)
            )
            carry = carry + jnp.sum(tiles[i], 1, keepdims=True)
        rank = jnp.concatenate(ranks, 1)
        posrow[...] = jnp.broadcast_to(target * PER + rank, (8, T))
        at = iota((LANES, T), 0).astype(F32) == rank
        shards = to_shard.astype(BF16)
        slots = nt(shards, jnp.where(at, high, 0.0).astype(BF16)) * 32.0 + nt(
            shards, jnp.where(at, low, 0.0).astype(BF16)
        )
        slots = jnp.where(iota((NB, LANES), 1) < USED, slots, -1.0)
        for d in range(NB):
            info[d] = jnp.broadcast_to(slots[d : d + 1], (8, LANES))
        wait_barrier()
        exchange_start(*info_args)
        got_info[pl.ds(me.b, 1)] = info[pl.ds(me.b, 1)]

    xn[:, :, :, 1408:1536] = jnp.zeros((2, 4, 80, 128), BF16)
    @pl.loop(0, 8)
    def _(i):
        n = iota((LANES, E), 1)
        k = iota((LANES, E), 0) + i * LANES
        sel[rows(i, LANES), :] = onehot(k == (n & 127) * 8 + (n >> 7))

    @pl.loop(0, 4)
    def _(i):
        n = iota((LANES, E), 1)
        k = iota((LANES, E), 0) + i * LANES
        sel_end[rows(i, LANES), :] = onehot(k == ((n & 127) - 52) * 8 + (n >> 7))

    n = iota((80, 640), 1)
    g = iota((80, 640), 0)
    for dx in range(8):
        perm[dx * 80 : dx * 80 + 80, :] = onehot(n == g * 8 + dx)
    loads[0].wait()
    for i in range(4):
        lanes = slice(i * 256, i * 256 + 256)
        wq[:, lanes] = dot(perm[...], weight[:, lanes]).astype(BF16)
    eye = onehot(iota((PIECE, PIECE), 0) == iota((PIECE, PIECE), 1))

    def clear_padding():
        for s in range(4):
            pad = slice(s * PIECE + SENT, (s + 1) * PIECE)
            zero = jnp.zeros((PIECE - SENT, 256), BF16)
            from_left[pad, :] = zero
            from_right[pad, :] = zero
            zin[pad, :] = zero[:, 0:128]
            for c in range(4):
                for hh in range(2):
                    dg[c, hh, pad, :] = zero[:, 0:128]

    def patches(ch):
        for s in (2 * ch, 2 * ch + 1):
            loads[1 + s].wait()

            @pl.loop(0, 5)
            def _(pair):
                halves = []
                for j in range(2):
                    k = 2 * pair + j
                    at = ids[k]
                    halves.append((fields[s, k].astype(F32) - shift[at]) * scale[at])
                for p in range(2):
                    both = jnp.concatenate([q[8 * p : 8 * p + 8] for q in halves], 0)
                    xn[p, s, rows(pair, 16), 0:1440] = both.astype(BF16)

        x = [xn[p, 2 * ch : 2 * ch + 2].reshape(160, T) for p in range(2)]
        both = jnp.concatenate(x, 0)
        for i in range(4):
            out = slice(i * 256, i * 256 + 256)
            low = dot(both[:, 0:1024], sel[:, out]).astype(BF16)
            end = (
                dot(x[0][:, 1024:1536], sel[0:512, out])
                + dot(x[1][:, 1024:1536], sel_end[:, out])
            ).astype(BF16)
            for q in range(2):
                at = slice((2 * i + q) * 80, (2 * i + q) * 80 + 80)
                lanes = slice(q * 128, q * 128 + 128)
                for s in range(2):
                    base = (2 * ch + s) * PIECE
                    for p in range(2):
                        first = (2 * p + s) * 80
                        xt[at, base + p * 128 : base + p * 128 + 128] = low[
                            first : first + 80, lanes
                        ]
                    xt[at, base + 256 : base + 384] = end[s * 80 : s * 80 + 80, lanes]

    def partials(s):
        xrow[...] = nt(eye, xt[:, sample(s)]).astype(BF16)
        for j, ahead in ((0, 2), (1, 1), (2, 3), (3, 0)):
            at = lax.rem(me.x + ahead, 4)
            lanes = pl.ds(pl.multiple_of(at * 256, 256), 256)
            part[j, sample(s), :] = dot(xrow[...], wq[:, lanes]).astype(BF16)

    def start_x(s):
        for f in range(2):
            ahead, back = (me.right, me.left) if f == 0 else (me.left, me.right)
            at = half(s, f)
            send(remote(part.at[0, at], leg.at[at], leg_s.at[s, f], leg_r.at[s, f], ahead, me.b))
            src, into, sem = (part.at[2], from_right, right_r) if f == 0 else (
                part.at[1], from_left, left_r)
            send(remote(src.at[at], into.at[at], dir_s.at[s, f], sem.at[s, f], back, me.b))

    def pass_on(s):
        for f in range(2):
            ahead, back = (me.right, me.left) if f == 0 else (me.left, me.right)
            at = half(s, f)
            remote(part.at[0, at], leg.at[at], leg_s.at[s, f], leg_r.at[s, f],
                   back, me.b).wait_recv()
            j = 1 + f
            part[j, at, :] = (part[j, at, :].astype(F32) + leg[at, :].astype(F32)).astype(BF16)
            into, sem = (from_left, left_r) if f == 0 else (from_right, right_r)
            send(remote(part.at[j, at], into.at[at], comb_s.at[s, f], sem.at[s, f], ahead, me.b))

    def finish_x(s):
        for f in range(2):
            at = half(s, f)
            src = part.at[0, at]
            remote(src, from_left.at[at], dir_s.at[s, f], left_r.at[s, f],
                   me.left, me.b).wait_recv()
            remote(src, from_right.at[at], dir_s.at[s, f], right_r.at[s, f],
                   me.right, me.b).wait_recv()
        sl = sample(s)
        total = (
            part[3, sl, :].astype(F32) + from_left[sl, :].astype(F32)
        ) + from_right[sl, :].astype(F32)
        mine = jnp.where(me.h == 0, total[:, 0:128], total[:, 128:256])
        other = jnp.where(me.h == 0, total[:, 128:256], total[:, 0:128])
        zout[sl, :] = other.astype(BF16)
        send(remote(zout.at[sent(s)], zin.at[sent(s)], z_s.at[s], z_r.at[s], me.over, me.b))
        pre[sl, :] = mine

    def finish_z(s):
        remote(zout.at[sent(s)], zin.at[sent(s)], z_s.at[s], z_r.at[s], me.over, me.b).wait_recv()
        sl = sample(s)
        pre[sl, :] = pre[sl, :] + zin[sl, :].astype(F32) + jnp.concatenate(position, 0)

    cot_args = (
        me,
        lambda d: cot_out.at[rows(d, PER)],
        lambda s: cot_in.at[rows(s, PER)],
        cot_s,
        cot_r,
    )
    wide = iota((384, T), 1).astype(F32)

    def answer():
        gpad[1440:T, :] = jnp.zeros((T - 1440, LANES), BF16)
        gout_load.wait()
        exchange_wait_recv(*info_args)
        asked = jnp.concatenate([got_info[s][0:1] for s in range(NB)], 0)
        asked = jnp.concatenate([asked, jnp.zeros((LANES - NB, LANES), F32)], 0).T
        for i in range(4):
            at = jnp.concatenate([asked[0:PER, s : s + 1] for s in range(8 * i, 8 * i + 8)], 0)
            slotcol[i * 384 : i * 384 + 384, :] = jnp.broadcast_to(at, (384, LANES))
            cot_out[i * 384 : i * 384 + 384, :] = dot(onehot(at == wide), gpad[...]).astype(BF16)
        exchange_start(*cot_args)
        cot_in[rows(me.b, PER), :] = cot_out[rows(me.b, PER), :]

    def place_cot():
        exchange_wait_recv(*cot_args)
        for i in range(4):
            sl = slice(i * 384, i * 384 + 384)
            cot[sl, :] = dot(onehot(poscol[sl, 0:1] == wide), cot_in[...]).astype(BF16)

    def local_sums(s):
        sl = sample(s)
        lane = iota((PIECE, LANES), 1)
        lane = jnp.where(iota((PIECE, LANES), 0) < 256, lane, lane - 4)
        a = pre[sl, :]
        g = cot[sl, :].astype(F32) * gain
        block = jnp.zeros((PIECE, LANES), F32)
        for k, q in enumerate((a, a * a, g, g * a)):
            block = jnp.where(lane == k, jnp.sum(q, 1, keepdims=True), block)
        flat = block.T[0:8]
        packed[s, :, 0:128] = flat[:, 0:128] + flat[:, 256:384]
        packed[s, :, 128:256] = flat[:, 128:256]
        sums_in[s, pl.ds(me.v, 1)] = packed[s][None]
        for k in range(1, NV):
            send(remote(packed.at[s], sums_in.at[s, me.v], sum_s.at[s, k - 1],
                        sum_r.at[s, me.v], lax.rem(me.v + k, NV), me.b))

    def all_sums(s):
        for k in range(1, NV):
            src = lax.rem(me.v + NV - k, NV)
            remote(packed.at[s], sums_in.at[s, src], sum_s.at[s, k - 1], sum_r.at[s, src],
                   src, me.b).wait_recv()
        total = sums_in[s, 0]
        for k in range(1, NV):
            total = total + sums_in[s, k]
        return jnp.concatenate([total, jnp.zeros((120, 256), F32)], 0).T

    own = dg.at[0, me.h]
    over = dg.at[0, 1 - me.h]
    totals = [jnp.zeros((1, LANES), F32), jnp.zeros((1, LANES), F32)]

    def send_x(block, hh, s):
        at = sent(s)
        send(remote(block.at[at], dg.at[1, hh, at], dx_s.at[hh, s, 0], dr_r.at[hh, s],
                    me.right, me.b))
        send(remote(block.at[at], dg.at[2, hh, at], dx_s.at[hh, s, 1], dl_r.at[hh, s],
                    me.left, me.b))

    def norm(s):
        col = all_sums(s)
        sl = sample(s)
        s1, s2, sg, sq = [
            jnp.concatenate([col[:, k : k + 1], col[0:128, 4 + k : 5 + k]], 0) for k in range(4)
        ]
        mean = s1 / E
        inv = lax.rsqrt(s2 / E - mean * mean + EPS)
        xhat = (pre[sl, :] - mean) * inv
        up = cot[sl, :].astype(F32)
        along = inv * (sq - mean * sg) / E
        d = inv * (up * gain - sg / E - xhat * along)
        own[sl, :] = d.astype(BF16)
        send(remote(own.at[sent(s)], own.at[sent(s)], dz_s.at[s], dz_r.at[s], me.over, me.b))
        send_x(own, me.h, s)
        emb[sl, :] = (xhat * gain + bias).astype(BF16)
        totals[0] = totals[0] + jnp.sum(up * xhat, 0, keepdims=True)
        totals[1] = totals[1] + jnp.sum(up, 0, keepdims=True)

    def over_arrives(s):
        remote(own.at[sent(s)], over.at[sent(s)], dz_s.at[s], dz_r.at[s], me.over, me.b).wait_recv()
        send_x(over, 1 - me.h, s)

    def pass_d(hh, s):
        at = sent(s)
        src = dg.at[0, hh, at]
        remote(src, dg.at[1, hh, at], dx_s.at[hh, s, 0], dr_r.at[hh, s], me.left, me.b).wait_recv()
        at = half(s, 0)
        send(remote(dg.at[1, hh, at], dg.at[3, hh, at], df_s.at[hh, s, 0], df_r.at[hh, s, 0],
                    me.right, me.b))
        at = sent(s)
        remote(src, dg.at[2, hh, at], dx_s.at[hh, s, 1], dl_r.at[hh, s], me.right, me.b).wait_recv()
        at = half(s, 1)
        send(remote(dg.at[2, hh, at], dg.at[3, hh, at], df_s.at[hh, s, 1], df_r.at[hh, s, 1],
                    me.left, me.b))

    def await_d(samples):
        for s in samples:
            for hh in range(2):
                for f in range(2):
                    at = half(s, f)
                    remote(dg.at[0, hh, at], dg.at[3, hh, at], df_s.at[hh, s, f],
                           df_r.at[hh, s, f], me.left, me.b).wait_recv()

    tall = iota((384, T), 0).astype(F32)
    emb_args = (
        me,
        lambda d: emb_out.at[rows(d, PER)],
        lambda s: emb_in.at[rows(s, PER)],
        emb_s,
        emb_r,
    )

    def pick_emb():
        for i in range(4):
            hot = onehot(posrow[0:1, :] == tall + i * 384.0)
            emb_out[i * 384 : i * 384 + 384, :] = dot(hot, emb[...]).astype(BF16)

    def start_emb():
        exchange_start(*emb_args)
        emb_in[rows(me.b, PER), :] = emb_out[rows(me.b, PER), :]

    def place_emb():
        exchange_wait_recv(*emb_args)
        for i in range(3):
            hot = onehot(slotrow[0:1, :] == iota((480, T), 0).astype(F32) + i * 480.0)
            embed[i * 480 : i * 480 + 480, :] = dot(hot, emb_in[...]).astype(BF16)

    even = me.core == 0
    across = jnp.where(even, lax.rem(me.b + NB - 1, NB), lax.rem(me.b + 1, NB))
    mate = jnp.where(even, me.b + 1, me.b - 1)
    outer_copy = remote(outer, outer_in, t_s.at[0], t_r.at[0], me.v, across)
    chip_copy = remote(chip, chip_in, t_s.at[1], t_r.at[1], me.v, mate)

    def table_rows():
        mixes = mix_blocks(me, True)
        term = jnp.zeros((LANES, LANES), F32)
        for i in range(12):
            term = term + dot(mixes[i % 3], own[i * LANES : (i + 1) * LANES, :])
        outer[...] = jnp.where(even, term[0:48], term[64:112])
        inner[...] = jnp.where(even, term[64:112], term[0:48])
        send(outer_copy)

    def table_chip():
        outer_copy.wait_recv()
        at = iota((48, LANES), 0)
        both = inner[...] + outer_in[...]
        chip[...] = jnp.where(at == 45, totals[0], jnp.where(at == 46, totals[1], both))
        send(chip_copy)

    def table_z():
        chip_copy.wait_recv()
        tables[pl.ds(me.y, 1), pl.ds(me.zl, 1)] = (chip[...] + chip_in[...])[None, None]
        for k in range(1, 4):
            to = lax.rem(me.zl + k, 4)
            here = tables.at[me.y, me.zl]
            send(remote(here, here, tz_s.at[k - 1], tz_r.at[k - 1],
                        me.v, to * 8 + me.y * 2 + me.core))

    def table_y():
        for k in range(1, 4):
            src = lax.rem(me.zl + 4 - k, 4)
            there = tables.at[me.y, src]
            remote(there, there, tz_s.at[k - 1], tz_r.at[k - 1],
                   me.v, src * 8 + me.y * 2 + me.core).wait_recv()
        for k in range(1, 4):
            to = lax.rem(me.y + k, 4)
            here = tables.at[me.y]
            send(remote(here, here, ty_s.at[k - 1], ty_r.at[k - 1],
                        me.v, me.zl * 8 + to * 2 + me.core))

    def table_end():
        for k in range(1, 4):
            src = lax.rem(me.y + 4 - k, 4)
            there = tables.at[src]
            remote(there, there, ty_s.at[k - 1], ty_r.at[k - 1],
                   me.v, me.zl * 8 + src * 2 + me.core).wait_recv()
        gain_total = jnp.zeros((1, LANES), F32)
        bias_total = jnp.zeros((1, LANES), F32)
        for i in range(16):
            block = tables[i % 4, i // 4]
            grad_table[:, i, :] = block[0:45]
            gain_total = gain_total + block[45:46]
            bias_total = bias_total + block[46:47]
        grad_gain[...] = gain_total
        grad_bias[...] = bias_total

    mate_core = 1 - me.core

    late = slice(3 * PIECE, T)

    def early(c):
        right = jnp.concatenate([dg[c, 0, 0 : 3 * PIECE], dg[c, 1, 0 : 3 * PIECE]], 1)
        first[c] = dot(xb[:, 0 : 3 * PIECE], right)

    def multiply(c):
        right = jnp.concatenate([dg[c, 0, late], dg[c, 1, late]], 1)
        theirs = pl.ds(pl.multiple_of(mate_core * 320, 320), 320)
        core_out[c] = (first[c, theirs, :] + dot(xb[theirs, late], right)).astype(BF16)
        send(remote(core_out.at[c], core_in.at[c], core_s.at[c], core_r.at[c], me.v, mate))
        mine = pl.ds(pl.multiple_of(me.core * 320, 320), 320)
        gw[c] = first[c, mine, :] + dot(xb[mine, late], right)

    def over_y(c):
        remote(core_out.at[c], core_in.at[c], core_s.at[c], core_r.at[c], me.v, mate).wait_recv()
        y_out[c] = (gw[c] + core_in[c].astype(F32)).astype(BF16)
        for k in range(1, 4):
            to = lax.rem(me.y + k, 4)
            src = y_out.at[c, rows(to, 80)]
            send(remote(src, y_in.at[c, k - 1], y_s.at[c, k - 1], y_r.at[c, k - 1],
                        me.v, me.zl * 8 + to * 2 + me.core))

    spread_r = iota((128, 80), 0)
    spread_c = iota((128, 80), 1)
    inside = spread_r & 31
    spread = onehot(
        jnp.logical_and(inside < 20, spread_c == (spread_r >> 5) * 20 + inside)
    )

    def over_z(c):
        total = y_out[c, rows(me.y, 80), :].astype(F32)
        for k in range(1, 4):
            src = lax.rem(me.y + 4 - k, 4)
            remote(y_out.at[c, rows(src, 80)], y_in.at[c, k - 1], y_s.at[c, k - 1],
                   y_r.at[c, k - 1], me.v, me.zl * 8 + src * 2 + me.core).wait_recv()
            total = total + y_in[c, k - 1].astype(F32)
        zl_out[c] = dot(spread, total.astype(BF16)).astype(BF16)
        for k in range(1, 4):
            to = lax.rem(me.zl + k, 4)
            send(remote(zl_out.at[c, rows(to, 32)], zl_in.at[c, k - 1], zl_s.at[c, k - 1],
                        zl_r.at[c, k - 1], me.v, to * 8 + me.y * 2 + me.core))

    def finish(c):
        total = zl_out[c, rows(me.zl, 32), :].astype(F32)
        for k in range(1, 4):
            src = lax.rem(me.zl + 4 - k, 4)
            remote(zl_out.at[c, rows(src, 32)], zl_in.at[c, k - 1], zl_s.at[c, k - 1],
                   zl_r.at[c, k - 1], me.v, src * 8 + me.y * 2 + me.core).wait_recv()
            total = total + zl_in[c, k - 1].astype(F32)
        x = lax.rem(me.x + (0, 3, 1, 2)[c], 4)
        grad_weight[:, pl.ds(pl.multiple_of(x * 256, 256), 256)] = total[0:20]

    ask()
    patches(0)
    partials(0)
    start_x(0)
    clear_padding()
    partials(1)
    start_x(1)
    answer()
    pass_on(0)
    patches(1)
    partials(2)
    start_x(2)
    pass_on(1)
    partials(3)
    start_x(3)

    low_row = (me.b + 1) // 2 - 1
    window[...] = jnp.zeros((LANES, LANES), F32)
    level = iota((45, 16, LANES), 1)
    table_load.wait()
    all_rows = table[...]
    window[0:45, :] = jnp.sum(jnp.where(level == low_row, all_rows, 0.0), 1)
    window[64:109, :] = jnp.sum(jnp.where(level == low_row + 1, all_rows, 0.0), 1)
    position = [
        jnp.dot(m.astype(F32), window[...], precision=HI, preferred_element_type=F32)
        for m in mix_blocks(me, False)
    ]
    poscol[...] = jnp.concatenate([posrow[...], jnp.zeros((120, T), F32)], 0).T

    finish_x(0)
    pass_on(2)

    r = iota((640, 1), 0)

    def steps(a, size, count):
        at = jnp.zeros_like(a)
        for i in range(1, count):
            at = at + jnp.where(a >= i * size, 1, 0)
        return at

    core = steps(r, 320, 2)
    r = r - 320 * core
    y = steps(r, 80, 4)
    r = r - 80 * y
    zl = steps(r, 20, 4)
    n = 20 * (zl * 8 + y * 2 + core) + r - 20 * zl
    permb[...] = onehot(iota((640, 640), 1) == (n & 7) * 80 + (n >> 3))

    def arrange(s):
        xb[:, sample(s)] = dot(permb[...], xt[:, sample(s)]).astype(BF16)

    arrange(0)
    finish_x(1)
    pass_on(3)
    arrange(1)
    place_cot()
    finish_x(2)
    finish_z(0)
    local_sums(0)
    finish_x(3)
    finish_z(1)
    local_sums(1)
    finish_z(2)
    local_sums(2)
    finish_z(3)
    local_sums(3)
    norm(0)
    norm(1)
    arrange(2)
    arrange(3)
    norm(2)
    norm(3)
    pass_d(me.h, 0)
    pass_d(me.h, 1)
    over_arrives(0)
    over_arrives(1)
    pass_d(1 - me.h, 0)
    pass_d(1 - me.h, 1)
    for i in range(12):
        sl = slice(i * LANES, (i + 1) * LANES)
        slotrow[:, sl] = slotcol[sl, :].T[0:8]
    pick_emb()
    over_arrives(2)
    pass_d(me.h, 2)
    early(0)
    table_rows()
    over_arrives(3)
    pass_d(me.h, 3)
    start_emb()
    multiply(0)
    pass_d(1 - me.h, 2)
    early(1)
    over_y(0)
    table_chip()
    early(2)
    pass_d(1 - me.h, 3)
    multiply(1)
    multiply(2)
    await_d(range(3))
    early(3)
    over_z(0)
    over_y(1)
    over_y(2)
    table_z()
    await_d(range(3, 4))
    multiply(3)
    over_z(1)
    over_z(2)
    over_y(3)
    table_y()
    finish(0)
    place_emb()
    over_z(3)
    finish(1)
    finish(2)
    table_end()
    finish(3)
    for copy in sends:
        copy.wait_send()
    exchange_wait_send(*info_args)
    exchange_wait_send(*cot_args)
    exchange_wait_send(*emb_args)


def result_kernel(*refs):
    count = len(refs) // 2
    for i in range(count):
        refs[count + i][...] = refs[i][...]


def dma(*shape):
    return pltpu.SemaphoreType.DMA(shape)


def vmem(shape, dtype=BF16):
    return pltpu.VMEM(shape, dtype)


def on_device(
    fields, var_ids, var_shift, var_scale, patch_weight, pos_table,
    layer_norm_gain, layer_norm_bias, order, grad_out,
):
    here = pl.BlockSpec(memory_space=pltpu.VMEM)
    scalars = pl.BlockSpec(memory_space=pltpu.SMEM)
    anywhere = pl.BlockSpec(memory_space=pl.ANY)
    shape = jax.ShapeDtypeStruct
    out_shape = (
        shape((1440, LANES), BF16),
        shape((20, E), F32),
        shape((45, 16, LANES), F32),
        shape((1, LANES), F32),
        shape((1, LANES), F32),
    )
    results = pl.pallas_call(
        encoder_kernel,
        out_shape=out_shape,
        in_specs=[scalars] * 3 + [anywhere] * 4 + [here] * 3,
        out_specs=(here,) * 5,
        scratch_shapes=[
            vmem((4, 10, 16, 1440)), vmem((640, E)), vmem((45, 16, LANES), F32),
            vmem((NB, 8, LANES), F32), vmem((NB, 8, LANES), F32), vmem((T, LANES), F32),
            vmem((8, T), F32), vmem((T, LANES), F32), vmem((8, T), F32),
            vmem((T, LANES)), vmem((T, LANES)), vmem((T, LANES)), vmem((T, LANES)),
            vmem((2, 4, 80, T)), vmem((E, E)), vmem((512, E)),
            vmem((640, 640)), vmem((640, 640)), vmem((640, T)), vmem((640, T)),
            vmem((PIECE, 640)), vmem((640, E)),
            vmem((4, T, 256)), vmem((T, 256)), vmem((T, 256)), vmem((T, 256)),
            vmem((T, LANES)), vmem((T, LANES)), vmem((LANES, LANES), F32), vmem((T, LANES), F32),
            vmem((4, 8, 256), F32), vmem((4, NV, 8, 256), F32),
            vmem((T, LANES)), vmem((T, LANES)), vmem((T, LANES)), vmem((4, 2, T, LANES)),
            vmem((4, 640, 256), F32),
            vmem((4, 320, 256)), vmem((4, 320, 256)), vmem((4, 320, 256), F32),
            vmem((4, 320, 256)), vmem((4, 3, 80, 256)),
            vmem((4, 128, 256)), vmem((4, 3, 32, 256)),
            vmem((48, LANES), F32), vmem((48, LANES), F32), vmem((48, LANES), F32),
            vmem((48, LANES), F32), vmem((48, LANES), F32), vmem((4, 4, 48, LANES), F32),
            dma(10), dma(NB), dma(NB), dma(NB), dma(NB),
            dma(4, 2), dma(4, 2), dma(4, 2), dma(4, 2), dma(4, 2), dma(4, 2), dma(4), dma(4),
            dma(4, 7), dma(4, NV), dma(NB), dma(NB), dma(4), dma(4),
            dma(2, 4, 2), dma(2, 4), dma(2, 4), dma(2, 4, 2), dma(2, 4, 2),
            dma(4), dma(4), dma(4, 3), dma(4, 3), dma(4, 3), dma(4, 3),
            dma(2), dma(2), dma(3), dma(3), dma(3), dma(3),
        ],
        compiler_params=pltpu.CompilerParams(
            has_side_effects=True, vmem_limit_bytes=58 * 1024 * 1024, collective_id=0
        ),
        name="encoder",
    )(
        var_ids, var_shift, var_scale, fields, patch_weight.reshape(640, E),
        pos_table.transpose(1, 0, 2), grad_out, order,
        layer_norm_gain.reshape(1, LANES), layer_norm_bias.reshape(1, LANES),
    )
    embed, grad_weight, grad_table, grad_gain, grad_bias = pl.pallas_call(
        result_kernel,
        out_shape=out_shape,
        in_specs=[here] * 5,
        out_specs=(here,) * 5,
        name="results",
    )(*results)
    return (
        embed, grad_weight, grad_table.transpose(1, 0, 2),
        grad_gain.reshape(LANES), grad_bias.reshape(LANES),
    )


def solution(mesh):
    in_specs = (
        P(None, "var", "band", None),
        P("var"),
        P(),
        P(),
        P("var", None, None),
        P(None, None, "var"),
        P("var"),
        P("var"),
        P("band"),
        P("band", "var"),
    )
    out_specs = (
        P("band", "var"),
        P(("var", "band"), None),
        P(None, None, "var"),
        P("var"),
        P("var"),
    )
    return jax.shard_map(
        on_device, mesh=mesh, in_specs=in_specs, out_specs=out_specs, check_vma=False
    )
```

```python
import functools

import jax
import jax.numpy as jnp
from jax import lax
from jax.experimental import pallas as pl
from jax.experimental.pallas import tpu as pltpu
from jax.sharding import PartitionSpec as P

EPS = 1e-05
T = 1536
LANES = 128
NB = 32
NV = 8
PER = 48
USED = 45
E = 1024
PIECE = 384
SENT = 368
F32 = jnp.float32
BF16 = jnp.bfloat16
HI = lax.Precision.HIGHEST


def iota(shape, dim):
    return lax.broadcasted_iota(jnp.int32, shape, dim)


def onehot(cond):
    return jnp.where(cond, 1.0, 0.0).astype(BF16)


def dot(a, b):
    return jnp.dot(a, b, preferred_element_type=F32)


def remote(src, dst, send, recv, v, b):
    return pltpu.make_async_remote_copy(
        src_ref=src,
        dst_ref=dst,
        send_sem=send,
        recv_sem=recv,
        device_id=(v, b),
        device_id_type=pl.DeviceIdType.MESH,
    )


class Place:
    def __init__(self):
        self.v = lax.axis_index("var")
        self.b = lax.axis_index("band")
        self.x = self.v // 2
        self.h = self.v % 2
        self.zl = self.b // 8
        self.y = (self.b // 2) % 4
        self.core = self.b % 2
        self.right = lax.rem(self.x + 1, 4) * 2 + self.h
        self.left = lax.rem(self.x + 3, 4) * 2 + self.h
        self.over = self.x * 2 + 1 - self.h

    def band_peer(self, k):
        return lax.rem(self.b + k, NB)

    def band_source(self, k):
        return lax.rem(self.b + NB - k, NB)


def greet(me, var_peers):
    barrier = pltpu.get_barrier_semaphore()

    @pl.loop(1, NB)
    def _(k):
        pl.semaphore_signal(
            barrier, inc=1, device_id=(me.v, me.band_peer(k)), device_id_type=pl.DeviceIdType.MESH
        )

    for peer in var_peers:
        pl.semaphore_signal(
            barrier, inc=1, device_id=(peer, me.b), device_id_type=pl.DeviceIdType.MESH
        )
    return lambda: pl.semaphore_wait(barrier, NB - 1 + len(var_peers))


def rows(i, n):
    return pl.ds(pl.multiple_of(i * n, n), n)


def exchange_start(me, src, dst, send, recv):
    @pl.loop(1, NB)
    def _(k):
        d = me.band_peer(k)
        remote(src(d), dst(me.b), send.at[d], recv.at[me.b], me.v, d).start()


def exchange_wait_recv(me, src, dst, send, recv):
    @pl.loop(1, NB)
    def _(k):
        s = me.band_source(k)
        remote(src(s), dst(s), send.at[s], recv.at[s], me.v, s).wait_recv()


def exchange_wait_send(me, src, dst, send, recv):
    @pl.loop(1, NB)
    def _(k):
        d = me.band_peer(k)
        remote(src(d), dst(d), send.at[d], recv.at[d], me.v, d).wait_send()


def mix_blocks(me, transposed):
    shape = (LANES, LANES)
    token = iota(shape, 1 if transposed else 0)
    cell = iota(shape, 0 if transposed else 1)
    second = cell >= 64
    j = jnp.where(second, cell - 64, cell)
    first = (me.b + 1) // 2 - 1

    def lat(p):
        u = jnp.clip(
            ((2 * me.b + p).astype(F32) + 0.5) / 4.0 - 0.5, 0.0, 15.0
        )
        w0 = jnp.maximum(1.0 - jnp.abs(u - first.astype(F32)), 0.0)
        w1 = jnp.maximum(1.0 - jnp.abs(u - (first + 1).astype(F32)), 0.0)
        return jnp.where(second, w1, w0)

    def lon(c):
        w = (c.astype(F32) + 0.5) / 4.0 - 0.5
        d = jnp.abs(w - j.astype(F32))
        d = jnp.minimum(d, 45.0 - d)
        return jnp.where(j < 45, jnp.maximum(1.0 - d, 0.0), 0.0)

    lat0, lat1 = lat(0), lat(1)
    low = lon(token)
    end0 = jnp.where(token < 52, lat0 * lon(token + 128), 0.0)
    end1 = jnp.where(
        jnp.logical_and(token >= 52, token < 104), lat1 * lon(token + 76), 0.0
    )
    return [(m).astype(BF16) for m in (lat0 * low, lat1 * low, end0 + end1)]


def nt(a, b):
    return lax.dot_general(a, b, (((1,), (1,)), ((), ())), preferred_element_type=F32)


def sample(s):
    return pl.ds(s * PIECE, PIECE)


def sent(s):
    return pl.ds(s * PIECE, SENT)


def half(s, f):
    return pl.ds(s * PIECE + 192 * f, 192 - 16 * f)


def encoder_kernel(
    ids, shift, scale, fields_at, weight_at, table_at, gout_at, order, gain_in, bias_in,
    embed, grad_weight, grad_table, grad_gain, grad_bias,
    fields, weight, table, info, got_info, slotcol, posrow, poscol, slotrow, gpad, cot_out, cot_in, cot,
    xn, sel, sel_end, perm, permb, xt, xb, xrow, wq, part, leg, from_left, from_right,
    zout, zin, window, pre,
    packed, sums_in, emb, emb_out, emb_in, dg,
    first, core_out, core_in, gw, y_out, y_in, zl_out, zl_in,
    outer, outer_in, inner, chip, chip_in, tables,
    load_s, info_s, info_r, cot_s, cot_r, leg_s, leg_r, dir_s, comb_s, left_r, right_r, z_s, z_r,
    sum_s, sum_r, emb_s, emb_r, dz_s, dz_r, dx_s, dr_r, dl_r, df_s, df_r,
    core_s, core_r, y_s, y_r, zl_s, zl_r, t_s, t_r, tz_s, tz_r, ty_s, ty_r,
):
    me = Place()
    wait_barrier = greet(me, [lax.rem(me.v + k, NV) for k in range(1, NV)])
    gain = gain_in[...]
    bias = bias_in[...]
    sends = []

    def send(copy):
        copy.start()
        sends.append(copy)

    loads = [pltpu.make_async_copy(weight_at, weight, load_s.at[4])]
    for s in range(4):
        loads.append(pltpu.make_async_copy(fields_at.at[s], fields.at[s], load_s.at[s]))
    for copy in loads:
        copy.start()
    gout_load = pltpu.make_async_copy(gout_at, gpad.at[pl.ds(0, 1440)], load_s.at[5])
    table_load = pltpu.make_async_copy(table_at, table, load_s.at[6])
    gout_load.start()
    table_load.start()

    info_args = (me, lambda d: info.at[d], lambda s: got_info.at[s], info_s, info_r)

    def ask():
        o = order[...].reshape(1, 1440).astype(F32)
        pieces = []
        for s in range(4):
            at = 360 * s
            pieces += [o[:, at : at + 128], o[:, at + 180 : at + 308]]
            pieces.append(
                jnp.concatenate(
                    [o[:, at + 128 : at + 180], o[:, at + 308 : at + 360],
                     jnp.full((1, 24), 99.0 * 1440.0, F32)], 1
                )
            )
        o = jnp.concatenate(pieces, 1)
        target = jnp.floor((o + 0.5) * (1.0 / 1440.0))
        slot = o - target * 1440.0
        high = jnp.floor(slot * (1.0 / 32.0))
        low = slot - high * 32.0
        to_shard = jnp.where(iota((NB, T), 0).astype(F32) == target, 1.0, 0.0)
        tiles = [to_shard[:, i * 128 : i * 128 + 128] for i in range(12)]
        above = onehot(iota((LANES, LANES), 0) < iota((LANES, LANES), 1))
        before = dot(jnp.concatenate(tiles, 0).astype(BF16), above)
        carry = jnp.zeros((NB, 1), F32)
        ranks = []
        for i in range(12):
            ranks.append(
                jnp.sum(tiles[i] * (before[i * NB : i * NB + NB] + carry), 0, keepdims=True)
            )
            carry = carry + jnp.sum(tiles[i], 1, keepdims=True)
        rank = jnp.concatenate(ranks, 1)
        posrow[...] = jnp.broadcast_to(target * PER + rank, (8, T))
        at = iota((LANES, T), 0).astype(F32) == rank
        shards = to_shard.astype(BF16)
        slots = nt(shards, jnp.where(at, high, 0.0).astype(BF16)) * 32.0 + nt(
            shards, jnp.where(at, low, 0.0).astype(BF16)
        )
        slots = jnp.where(iota((NB, LANES), 1) < USED, slots, -1.0)
        for d in range(NB):
            info[d] = jnp.broadcast_to(slots[d : d + 1], (8, LANES))
        wait_barrier()
        exchange_start(*info_args)
        got_info[pl.ds(me.b, 1)] = info[pl.ds(me.b, 1)]

    xn[:, :, :, 1408:1536] = jnp.zeros((2, 4, 80, 128), BF16)
    @pl.loop(0, 8)
    def _(i):
        n = iota((LANES, E), 1)
        k = iota((LANES, E), 0) + i * LANES
        sel[rows(i, LANES), :] = onehot(k == (n & 127) * 8 + (n >> 7))

    @pl.loop(0, 4)
    def _(i):
        n = iota((LANES, E), 1)
        k = iota((LANES, E), 0) + i * LANES
        sel_end[rows(i, LANES), :] = onehot(k == ((n & 127) - 52) * 8 + (n >> 7))

    n = iota((80, 640), 1)
    g = iota((80, 640), 0)
    for dx in range(8):
        perm[dx * 80 : dx * 80 + 80, :] = onehot(n == g * 8 + dx)
    loads[0].wait()
    for i in range(4):
        lanes = slice(i * 256, i * 256 + 256)
        wq[:, lanes] = dot(perm[...], weight[:, lanes]).astype(BF16)
    eye = onehot(iota((PIECE, PIECE), 0) == iota((PIECE, PIECE), 1))

    def clear_padding():
        for s in range(4):
            pad = slice(s * PIECE + SENT, (s + 1) * PIECE)
            zero = jnp.zeros((PIECE - SENT, 256), BF16)
            from_left[pad, :] = zero
            from_right[pad, :] = zero
            zin[pad, :] = zero[:, 0:128]
            for c in range(4):
                for hh in range(2):
                    dg[c, hh, pad, :] = zero[:, 0:128]

    def patches(ch):
        for s in (2 * ch, 2 * ch + 1):
            loads[1 + s].wait()

            @pl.loop(0, 5)
            def _(pair):
                halves = []
                for j in range(2):
                    k = 2 * pair + j
                    at = ids[k]
                    halves.append((fields[s, k].astype(F32) - shift[at]) * scale[at])
                for p in range(2):
                    both = jnp.concatenate([q[8 * p : 8 * p + 8] for q in halves], 0)
                    xn[p, s, rows(pair, 16), 0:1440] = both.astype(BF16)

        x = [xn[p, 2 * ch : 2 * ch + 2].reshape(160, T) for p in range(2)]
        both = jnp.concatenate(x, 0)
        for i in range(4):
            out = slice(i * 256, i * 256 + 256)
            low = dot(both[:, 0:1024], sel[:, out]).astype(BF16)
            end = (
                dot(x[0][:, 1024:1536], sel[0:512, out])
                + dot(x[1][:, 1024:1536], sel_end[:, out])
            ).astype(BF16)
            for q in range(2):
                at = slice((2 * i + q) * 80, (2 * i + q) * 80 + 80)
                lanes = slice(q * 128, q * 128 + 128)
                for s in range(2):
                    base = (2 * ch + s) * PIECE
                    for p in range(2):
                        first = (2 * p + s) * 80
                        xt[at, base + p * 128 : base + p * 128 + 128] = low[
                            first : first + 80, lanes
                        ]
                    xt[at, base + 256 : base + 384] = end[s * 80 : s * 80 + 80, lanes]

    def partials(s):
        xrow[...] = nt(eye, xt[:, sample(s)]).astype(BF16)
        for j, ahead in ((0, 2), (1, 1), (2, 3), (3, 0)):
            at = lax.rem(me.x + ahead, 4)
            lanes = pl.ds(pl.multiple_of(at * 256, 256), 256)
            part[j, sample(s), :] = dot(xrow[...], wq[:, lanes]).astype(BF16)

    def start_x(s):
        for f in range(2):
            ahead, back = (me.right, me.left) if f == 0 else (me.left, me.right)
            at = half(s, f)
            send(remote(part.at[0, at], leg.at[at], leg_s.at[s, f], leg_r.at[s, f], ahead, me.b))
            src, into, sem = (part.at[2], from_right, right_r) if f == 0 else (
                part.at[1], from_left, left_r)
            send(remote(src.at[at], into.at[at], dir_s.at[s, f], sem.at[s, f], back, me.b))

    def pass_on(s):
        for f in range(2):
            ahead, back = (me.right, me.left) if f == 0 else (me.left, me.right)
            at = half(s, f)
            remote(part.at[0, at], leg.at[at], leg_s.at[s, f], leg_r.at[s, f],
                   back, me.b).wait_recv()
            j = 1 + f
            part[j, at, :] = (part[j, at, :].astype(F32) + leg[at, :].astype(F32)).astype(BF16)
            into, sem = (from_left, left_r) if f == 0 else (from_right, right_r)
            send(remote(part.at[j, at], into.at[at], comb_s.at[s, f], sem.at[s, f], ahead, me.b))

    def finish_x(s):
        for f in range(2):
            at = half(s, f)
            src = part.at[0, at]
            remote(src, from_left.at[at], dir_s.at[s, f], left_r.at[s, f],
                   me.left, me.b).wait_recv()
            remote(src, from_right.at[at], dir_s.at[s, f], right_r.at[s, f],
                   me.right, me.b).wait_recv()
        sl = sample(s)
        total = (
            part[3, sl, :].astype(F32) + from_left[sl, :].astype(F32)
        ) + from_right[sl, :].astype(F32)
        mine = jnp.where(me.h == 0, total[:, 0:128], total[:, 128:256])
        other = jnp.where(me.h == 0, total[:, 128:256], total[:, 0:128])
        zout[sl, :] = other.astype(BF16)
        send(remote(zout.at[sent(s)], zin.at[sent(s)], z_s.at[s], z_r.at[s], me.over, me.b))
        pre[sl, :] = mine

    def finish_z(s):
        remote(zout.at[sent(s)], zin.at[sent(s)], z_s.at[s], z_r.at[s], me.over, me.b).wait_recv()
        sl = sample(s)
        pre[sl, :] = pre[sl, :] + zin[sl, :].astype(F32) + jnp.concatenate(position, 0)

    cot_args = (
        me,
        lambda d: cot_out.at[rows(d, PER)],
        lambda s: cot_in.at[rows(s, PER)],
        cot_s,
        cot_r,
    )
    wide = iota((384, T), 1).astype(F32)

    def answer():
        gpad[1440:T, :] = jnp.zeros((T - 1440, LANES), BF16)
        gout_load.wait()
        exchange_wait_recv(*info_args)
        asked = jnp.concatenate([got_info[s][0:1] for s in range(NB)], 0)
        asked = jnp.concatenate([asked, jnp.zeros((LANES - NB, LANES), F32)], 0).T
        for i in range(4):
            at = jnp.concatenate([asked[0:PER, s : s + 1] for s in range(8 * i, 8 * i + 8)], 0)
            slotcol[i * 384 : i * 384 + 384, :] = jnp.broadcast_to(at, (384, LANES))
            cot_out[i * 384 : i * 384 + 384, :] = dot(onehot(at == wide), gpad[...]).astype(BF16)
        exchange_start(*cot_args)
        cot_in[rows(me.b, PER), :] = cot_out[rows(me.b, PER), :]

    def place_cot():
        exchange_wait_recv(*cot_args)
        for i in range(4):
            sl = slice(i * 384, i * 384 + 384)
            cot[sl, :] = dot(onehot(poscol[sl, 0:1] == wide), cot_in[...]).astype(BF16)

    def local_sums(s):
        sl = sample(s)
        lane = iota((PIECE, LANES), 1)
        lane = jnp.where(iota((PIECE, LANES), 0) < 256, lane, lane - 4)
        a = pre[sl, :]
        g = cot[sl, :].astype(F32) * gain
        block = jnp.zeros((PIECE, LANES), F32)
        for k, q in enumerate((a, a * a, g, g * a)):
            block = jnp.where(lane == k, jnp.sum(q, 1, keepdims=True), block)
        flat = block.T[0:8]
        packed[s, :, 0:128] = flat[:, 0:128] + flat[:, 256:384]
        packed[s, :, 128:256] = flat[:, 128:256]
        sums_in[s, pl.ds(me.v, 1)] = packed[s][None]
        for k in range(1, NV):
            send(remote(packed.at[s], sums_in.at[s, me.v], sum_s.at[s, k - 1],
                        sum_r.at[s, me.v], lax.rem(me.v + k, NV), me.b))

    def all_sums(s):
        for k in range(1, NV):
            src = lax.rem(me.v + NV - k, NV)
            remote(packed.at[s], sums_in.at[s, src], sum_s.at[s, k - 1], sum_r.at[s, src],
                   src, me.b).wait_recv()
        total = sums_in[s, 0]
        for k in range(1, NV):
            total = total + sums_in[s, k]
        return jnp.concatenate([total, jnp.zeros((120, 256), F32)], 0).T

    own = dg.at[0, me.h]
    over = dg.at[0, 1 - me.h]
    totals = [jnp.zeros((1, LANES), F32), jnp.zeros((1, LANES), F32)]

    def send_x(block, hh, s):
        at = sent(s)
        send(remote(block.at[at], dg.at[1, hh, at], dx_s.at[hh, s, 0], dr_r.at[hh, s],
                    me.right, me.b))
        send(remote(block.at[at], dg.at[2, hh, at], dx_s.at[hh, s, 1], dl_r.at[hh, s],
                    me.left, me.b))

    def norm(s):
        col = all_sums(s)
        sl = sample(s)
        s1, s2, sg, sq = [
            jnp.concatenate([col[:, k : k + 1], col[0:128, 4 + k : 5 + k]], 0) for k in range(4)
        ]
        mean = s1 / E
        inv = lax.rsqrt(s2 / E - mean * mean + EPS)
        xhat = (pre[sl, :] - mean) * inv
        up = cot[sl, :].astype(F32)
        along = inv * (sq - mean * sg) / E
        d = inv * (up * gain - sg / E - xhat * along)
        own[sl, :] = d.astype(BF16)
        send(remote(own.at[sent(s)], own.at[sent(s)], dz_s.at[s], dz_r.at[s], me.over, me.b))
        send_x(own, me.h, s)
        emb[sl, :] = (xhat * gain + bias).astype(BF16)
        totals[0] = totals[0] + jnp.sum(up * xhat, 0, keepdims=True)
        totals[1] = totals[1] + jnp.sum(up, 0, keepdims=True)

    def over_arrives(s):
        remote(own.at[sent(s)], over.at[sent(s)], dz_s.at[s], dz_r.at[s], me.over, me.b).wait_recv()
        send_x(over, 1 - me.h, s)

    def pass_d(hh, s):
        at = sent(s)
        src = dg.at[0, hh, at]
        remote(src, dg.at[1, hh, at], dx_s.at[hh, s, 0], dr_r.at[hh, s], me.left, me.b).wait_recv()
        at = half(s, 0)
        send(remote(dg.at[1, hh, at], dg.at[3, hh, at], df_s.at[hh, s, 0], df_r.at[hh, s, 0],
                    me.right, me.b))
        at = sent(s)
        remote(src, dg.at[2, hh, at], dx_s.at[hh, s, 1], dl_r.at[hh, s], me.right, me.b).wait_recv()
        at = half(s, 1)
        send(remote(dg.at[2, hh, at], dg.at[3, hh, at], df_s.at[hh, s, 1], df_r.at[hh, s, 1],
                    me.left, me.b))

    def await_d(samples):
        for s in samples:
            for hh in range(2):
                for f in range(2):
                    at = half(s, f)
                    remote(dg.at[0, hh, at], dg.at[3, hh, at], df_s.at[hh, s, f],
                           df_r.at[hh, s, f], me.left, me.b).wait_recv()

    tall = iota((384, T), 0).astype(F32)
    emb_args = (
        me,
        lambda d: emb_out.at[rows(d, PER)],
        lambda s: emb_in.at[rows(s, PER)],
        emb_s,
        emb_r,
    )

    def pick_emb():
        for i in range(4):
            hot = onehot(posrow[0:1, :] == tall + i * 384.0)
            emb_out[i * 384 : i * 384 + 384, :] = dot(hot, emb[...]).astype(BF16)

    def start_emb():
        exchange_start(*emb_args)
        emb_in[rows(me.b, PER), :] = emb_out[rows(me.b, PER), :]

    def place_emb():
        exchange_wait_recv(*emb_args)
        for i in range(3):
            hot = onehot(slotrow[0:1, :] == iota((480, T), 0).astype(F32) + i * 480.0)
            embed[i * 480 : i * 480 + 480, :] = dot(hot, emb_in[...]).astype(BF16)

    even = me.core == 0
    across = jnp.where(even, lax.rem(me.b + NB - 1, NB), lax.rem(me.b + 1, NB))
    mate = jnp.where(even, me.b + 1, me.b - 1)
    outer_copy = remote(outer, outer_in, t_s.at[0], t_r.at[0], me.v, across)
    chip_copy = remote(chip, chip_in, t_s.at[1], t_r.at[1], me.v, mate)

    def table_rows():
        mixes = mix_blocks(me, True)
        term = jnp.zeros((LANES, LANES), F32)
        for i in range(12):
            term = term + dot(mixes[i % 3], own[i * LANES : (i + 1) * LANES, :])
        outer[...] = jnp.where(even, term[0:48], term[64:112])
        inner[...] = jnp.where(even, term[64:112], term[0:48])
        send(outer_copy)

    def table_chip():
        outer_copy.wait_recv()
        at = iota((48, LANES), 0)
        both = inner[...] + outer_in[...]
        chip[...] = jnp.where(at == 45, totals[0], jnp.where(at == 46, totals[1], both))
        send(chip_copy)

    def table_z():
        chip_copy.wait_recv()
        tables[pl.ds(me.y, 1), pl.ds(me.zl, 1)] = (chip[...] + chip_in[...])[None, None]
        for k in range(1, 4):
            to = lax.rem(me.zl + k, 4)
            here = tables.at[me.y, me.zl]
            send(remote(here, here, tz_s.at[k - 1], tz_r.at[k - 1],
                        me.v, to * 8 + me.y * 2 + me.core))

    def table_y():
        for k in range(1, 4):
            src = lax.rem(me.zl + 4 - k, 4)
            there = tables.at[me.y, src]
            remote(there, there, tz_s.at[k - 1], tz_r.at[k - 1],
                   me.v, src * 8 + me.y * 2 + me.core).wait_recv()
        for k in range(1, 4):
            to = lax.rem(me.y + k, 4)
            here = tables.at[me.y]
            send(remote(here, here, ty_s.at[k - 1], ty_r.at[k - 1],
                        me.v, me.zl * 8 + to * 2 + me.core))

    def table_end():
        for k in range(1, 4):
            src = lax.rem(me.y + 4 - k, 4)
            there = tables.at[src]
            remote(there, there, ty_s.at[k - 1], ty_r.at[k - 1],
                   me.v, me.zl * 8 + src * 2 + me.core).wait_recv()
        gain_total = jnp.zeros((1, LANES), F32)
        bias_total = jnp.zeros((1, LANES), F32)
        for i in range(16):
            block = tables[i % 4, i // 4]
            grad_table[:, i, :] = block[0:45]
            gain_total = gain_total + block[45:46]
            bias_total = bias_total + block[46:47]
        grad_gain[...] = gain_total
        grad_bias[...] = bias_total

    mate_core = 1 - me.core

    late = slice(3 * PIECE, T)

    def early(c):
        right = jnp.concatenate([dg[c, 0, 0 : 3 * PIECE], dg[c, 1, 0 : 3 * PIECE]], 1)
        first[c] = dot(xb[:, 0 : 3 * PIECE], right)

    def multiply(c):
        right = jnp.concatenate([dg[c, 0, late], dg[c, 1, late]], 1)
        theirs = pl.ds(pl.multiple_of(mate_core * 320, 320), 320)
        core_out[c] = (first[c, theirs, :] + dot(xb[theirs, late], right)).astype(BF16)
        send(remote(core_out.at[c], core_in.at[c], core_s.at[c], core_r.at[c], me.v, mate))
        mine = pl.ds(pl.multiple_of(me.core * 320, 320), 320)
        gw[c] = first[c, mine, :] + dot(xb[mine, late], right)

    def over_y(c):
        remote(core_out.at[c], core_in.at[c], core_s.at[c], core_r.at[c], me.v, mate).wait_recv()
        y_out[c] = (gw[c] + core_in[c].astype(F32)).astype(BF16)
        for k in range(1, 4):
            to = lax.rem(me.y + k, 4)
            src = y_out.at[c, rows(to, 80)]
            send(remote(src, y_in.at[c, k - 1], y_s.at[c, k - 1], y_r.at[c, k - 1],
                        me.v, me.zl * 8 + to * 2 + me.core))

    spread_r = iota((128, 80), 0)
    spread_c = iota((128, 80), 1)
    inside = spread_r & 31
    spread = onehot(
        jnp.logical_and(inside < 20, spread_c == (spread_r >> 5) * 20 + inside)
    )

    def over_z(c):
        total = y_out[c, rows(me.y, 80), :].astype(F32)
        for k in range(1, 4):
            src = lax.rem(me.y + 4 - k, 4)
            remote(y_out.at[c, rows(src, 80)], y_in.at[c, k - 1], y_s.at[c, k - 1],
                   y_r.at[c, k - 1], me.v, me.zl * 8 + src * 2 + me.core).wait_recv()
            total = total + y_in[c, k - 1].astype(F32)
        zl_out[c] = dot(spread, total.astype(BF16)).astype(BF16)
        for k in range(1, 4):
            to = lax.rem(me.zl + k, 4)
            send(remote(zl_out.at[c, rows(to, 32)], zl_in.at[c, k - 1], zl_s.at[c, k - 1],
                        zl_r.at[c, k - 1], me.v, to * 8 + me.y * 2 + me.core))

    def finish(c):
        total = zl_out[c, rows(me.zl, 32), :].astype(F32)
        for k in range(1, 4):
            src = lax.rem(me.zl + 4 - k, 4)
            remote(zl_out.at[c, rows(src, 32)], zl_in.at[c, k - 1], zl_s.at[c, k - 1],
                   zl_r.at[c, k - 1], me.v, src * 8 + me.y * 2 + me.core).wait_recv()
            total = total + zl_in[c, k - 1].astype(F32)
        x = lax.rem(me.x + (0, 3, 1, 2)[c], 4)
        grad_weight[:, pl.ds(pl.multiple_of(x * 256, 256), 256)] = total[0:20]

    ask()
    patches(0)
    partials(0)
    start_x(0)
    clear_padding()
    partials(1)
    start_x(1)
    answer()
    pass_on(0)
    patches(1)
    partials(2)
    start_x(2)
    pass_on(1)
    partials(3)
    start_x(3)

    low_row = (me.b + 1) // 2 - 1
    window[...] = jnp.zeros((LANES, LANES), F32)
    level = iota((45, 16, LANES), 1)
    table_load.wait()
    all_rows = table[...]
    window[0:45, :] = jnp.sum(jnp.where(level == low_row, all_rows, 0.0), 1)
    window[64:109, :] = jnp.sum(jnp.where(level == low_row + 1, all_rows, 0.0), 1)
    position = [
        jnp.dot(m.astype(F32), window[...], precision=HI, preferred_element_type=F32)
        for m in mix_blocks(me, False)
    ]
    poscol[...] = jnp.concatenate([posrow[...], jnp.zeros((120, T), F32)], 0).T

    finish_x(0)
    pass_on(2)

    r = iota((640, 1), 0)

    def steps(a, size, count):
        at = jnp.zeros_like(a)
        for i in range(1, count):
            at = at + jnp.where(a >= i * size, 1, 0)
        return at

    core = steps(r, 320, 2)
    r = r - 320 * core
    y = steps(r, 80, 4)
    r = r - 80 * y
    zl = steps(r, 20, 4)
    n = 20 * (zl * 8 + y * 2 + core) + r - 20 * zl
    permb[...] = onehot(iota((640, 640), 1) == (n & 7) * 80 + (n >> 3))

    def arrange(s):
        xb[:, sample(s)] = dot(permb[...], xt[:, sample(s)]).astype(BF16)

    arrange(0)
    finish_x(1)
    pass_on(3)
    arrange(1)
    finish_x(2)
    place_cot()
    finish_z(0)
    local_sums(0)
    finish_x(3)
    finish_z(1)
    local_sums(1)
    finish_z(2)
    local_sums(2)
    finish_z(3)
    local_sums(3)
    norm(0)
    norm(1)
    arrange(2)
    arrange(3)
    norm(2)
    norm(3)
    pass_d(me.h, 0)
    pass_d(me.h, 1)
    over_arrives(0)
    over_arrives(1)
    pass_d(1 - me.h, 0)
    pass_d(1 - me.h, 1)
    for i in range(12):
        sl = slice(i * LANES, (i + 1) * LANES)
        slotrow[:, sl] = slotcol[sl, :].T[0:8]
    pick_emb()
    over_arrives(2)
    pass_d(me.h, 2)
    early(0)
    table_rows()
    over_arrives(3)
    pass_d(me.h, 3)
    start_emb()
    multiply(0)
    pass_d(1 - me.h, 2)
    early(1)
    over_y(0)
    table_chip()
    early(2)
    pass_d(1 - me.h, 3)
    multiply(1)
    multiply(2)
    await_d(range(3))
    early(3)
    over_z(0)
    over_y(1)
    over_y(2)
    table_z()
    await_d(range(3, 4))
    multiply(3)
    over_z(1)
    over_z(2)
    over_y(3)
    table_y()
    finish(0)
    place_emb()
    over_z(3)
    finish(1)
    finish(2)
    table_end()
    finish(3)
    for copy in sends:
        copy.wait_send()
    exchange_wait_send(*info_args)
    exchange_wait_send(*cot_args)
    exchange_wait_send(*emb_args)


def result_kernel(*refs):
    count = len(refs) // 2
    for i in range(count):
        refs[count + i][...] = refs[i][...]


def dma(*shape):
    return pltpu.SemaphoreType.DMA(shape)


def vmem(shape, dtype=BF16):
    return pltpu.VMEM(shape, dtype)


def on_device(
    fields, var_ids, var_shift, var_scale, patch_weight, pos_table,
    layer_norm_gain, layer_norm_bias, order, grad_out,
):
    here = pl.BlockSpec(memory_space=pltpu.VMEM)
    scalars = pl.BlockSpec(memory_space=pltpu.SMEM)
    anywhere = pl.BlockSpec(memory_space=pl.ANY)
    shape = jax.ShapeDtypeStruct
    out_shape = (
        shape((1440, LANES), BF16),
        shape((20, E), F32),
        shape((45, 16, LANES), F32),
        shape((1, LANES), F32),
        shape((1, LANES), F32),
    )
    results = pl.pallas_call(
        encoder_kernel,
        out_shape=out_shape,
        in_specs=[scalars] * 3 + [anywhere] * 4 + [here] * 3,
        out_specs=(here,) * 5,
        scratch_shapes=[
            vmem((4, 10, 16, 1440)), vmem((640, E)), vmem((45, 16, LANES), F32),
            vmem((NB, 8, LANES), F32), vmem((NB, 8, LANES), F32), vmem((T, LANES), F32),
            vmem((8, T), F32), vmem((T, LANES), F32), vmem((8, T), F32),
            vmem((T, LANES)), vmem((T, LANES)), vmem((T, LANES)), vmem((T, LANES)),
            vmem((2, 4, 80, T)), vmem((E, E)), vmem((512, E)),
            vmem((640, 640)), vmem((640, 640)), vmem((640, T)), vmem((640, T)),
            vmem((PIECE, 640)), vmem((640, E)),
            vmem((4, T, 256)), vmem((T, 256)), vmem((T, 256)), vmem((T, 256)),
            vmem((T, LANES)), vmem((T, LANES)), vmem((LANES, LANES), F32), vmem((T, LANES), F32),
            vmem((4, 8, 256), F32), vmem((4, NV, 8, 256), F32),
            vmem((T, LANES)), vmem((T, LANES)), vmem((T, LANES)), vmem((4, 2, T, LANES)),
            vmem((4, 640, 256), F32),
            vmem((4, 320, 256)), vmem((4, 320, 256)), vmem((4, 320, 256), F32),
            vmem((4, 320, 256)), vmem((4, 3, 80, 256)),
            vmem((4, 128, 256)), vmem((4, 3, 32, 256)),
            vmem((48, LANES), F32), vmem((48, LANES), F32), vmem((48, LANES), F32),
            vmem((48, LANES), F32), vmem((48, LANES), F32), vmem((4, 4, 48, LANES), F32),
            dma(10), dma(NB), dma(NB), dma(NB), dma(NB),
            dma(4, 2), dma(4, 2), dma(4, 2), dma(4, 2), dma(4, 2), dma(4, 2), dma(4), dma(4),
            dma(4, 7), dma(4, NV), dma(NB), dma(NB), dma(4), dma(4),
            dma(2, 4, 2), dma(2, 4), dma(2, 4), dma(2, 4, 2), dma(2, 4, 2),
            dma(4), dma(4), dma(4, 3), dma(4, 3), dma(4, 3), dma(4, 3),
            dma(2), dma(2), dma(3), dma(3), dma(3), dma(3),
        ],
        compiler_params=pltpu.CompilerParams(
            has_side_effects=True, vmem_limit_bytes=58 * 1024 * 1024, collective_id=0
        ),
        name="encoder",
    )(
        var_ids, var_shift, var_scale, fields, patch_weight.reshape(640, E),
        pos_table.transpose(1, 0, 2), grad_out, order,
        layer_norm_gain.reshape(1, LANES), layer_norm_bias.reshape(1, LANES),
    )
    embed, grad_weight, grad_table, grad_gain, grad_bias = pl.pallas_call(
        result_kernel,
        out_shape=out_shape,
        in_specs=[here] * 5,
        out_specs=(here,) * 5,
        name="results",
    )(*results)
    return (
        embed, grad_weight, grad_table.transpose(1, 0, 2),
        grad_gain.reshape(LANES), grad_bias.reshape(LANES),
    )


def solution(mesh):
    in_specs = (
        P(None, "var", "band", None),
        P("var"),
        P(),
        P(),
        P("var", None, None),
        P(None, None, "var"),
        P("var"),
        P("var"),
        P("band"),
        P("band", "var"),
    )
    out_specs = (
        P("band", "var"),
        P(("var", "band"), None),
        P(None, None, "var"),
        P("var"),
        P("var"),
    )
    return jax.shard_map(
        on_device, mesh=mesh, in_specs=in_specs, out_specs=out_specs, check_vma=False
    )
```
